32 devices in a mesh: ctx: 8 (over y, x, core), fsdp: 4 (over z).
Axes of the slice: x: 2, y: 2, z: 4, core: 2. Of those that a mesh axis runs over, the one named last changes fastest.
Arguments:
- tokens: bfloat16 [4, 1536, 896], P('fsdp', 'ctx'), may hold values from -6 to 6
- cotangent: bfloat16 [4, 1536, 896], P('fsdp', 'ctx'), may hold values from -6 to 6
- doc_lengths: int32 [4, 4], P('fsdp'), may hold values from 1 to 1440, as said below
- w_attn_in: float32 [896, 1152], P('fsdp'), may hold values from -0.1875 to 0.1875
- w_attn_out: float32 [896, 896], P('fsdp'), may hold values from -3.5 to 3.5
- w_mlp_in: float32 [896, 9728], P('fsdp'), may hold values from -0.1875 to 0.1875
- w_mlp_out: float32 [4864, 896], P('fsdp'), may hold values from -0.078125 to 0.078125
- gains: float32 [2, 896], P(None, 'fsdp'), may hold values from 0.5 to 1.5
- biases: float32 [1152], P('fsdp'), may hold values from -0.12 to 0.12
- first_attn_in: float32 [896, 1152], P('fsdp'), may hold values from -172.44408 to 172.44408
- first_attn_out: float32 [896, 896], P('fsdp'), may hold values from -2.6944387 to 2.6944387
- first_mlp_in: float32 [896, 9728], P('fsdp'), may hold values from -10.973714 to 10.973714
- first_mlp_out: float32 [4864, 896], P('fsdp'), may hold values from -25.866611 to 25.866611
- first_gains: float32 [2, 896], P(None, 'fsdp'), may hold values from -129.33305 to 129.33305
- first_biases: float32 [1152], P('fsdp'), may hold values from -963.0229 to 963.0229
- second_attn_in: float32 [896, 1152], P('fsdp'), may hold values from 49.152 to 786.432
- second_attn_out: float32 [896, 896], P('fsdp'), may hold values from 0.012 to 0.192
- second_mlp_in: float32 [896, 9728], P('fsdp'), may hold values from 0.192 to 3.072
- second_mlp_out: float32 [4864, 896], P('fsdp'), may hold values from 1.10592 to 17.69472
- second_gains: float32 [2, 896], P(None, 'fsdp'), may hold values from 27.648 to 442.368
- second_biases: float32 [1152], P('fsdp'), may hold values from 49.152 to 205520.896
Outputs:
- output: bfloat16 [4, 1536, 896], P('fsdp', 'ctx')
- tokens_grad: float32 [4, 1536, 896], P('fsdp', 'ctx')
- new_attn_in: float32 [896, 1152], P('fsdp')
- moment_attn_in: float32 [896, 1152], P('fsdp')
- square_attn_in: float32 [896, 1152], P('fsdp')
- new_attn_out: float32 [896, 896], P('fsdp')
- moment_attn_out: float32 [896, 896], P('fsdp')
- square_attn_out: float32 [896, 896], P('fsdp')
- new_mlp_in: float32 [896, 9728], P('fsdp')
- moment_mlp_in: float32 [896, 9728], P('fsdp')
- square_mlp_in: float32 [896, 9728], P('fsdp')
- new_mlp_out: float32 [4864, 896], P('fsdp')
- moment_mlp_out: float32 [4864, 896], P('fsdp')
- square_mlp_out: float32 [4864, 896], P('fsdp')
- new_gains: float32 [2, 896], P(None, 'fsdp')
- moment_gains: float32 [2, 896], P(None, 'fsdp')
- square_gains: float32 [2, 896], P(None, 'fsdp')
- new_biases: float32 [1152], P('fsdp')
- moment_biases: float32 [1152], P('fsdp')
- square_biases: float32 [1152], P('fsdp')
The draws below stay inside these ranges and needn't reach their ends.
Inputs may be any that keep to these rules, and one draw needn't show every extreme that they name: `doc_lengths`: every row sums to 1536; one document per row has exactly 1440 tokens and the others together 192 // 2, each at least one.
All inputs are finite; a program needn't handle non-finite values.
Results may differ from the reference program's by a relative error of at most 0.014.
Values may be sent and summed in bfloat16 or wider, within the bound.
A program may use at most 320 MiB of HBM per device.

```python
import math
import jax
import jax.numpy as jnp
from jax import lax

D = 896
QUERY_HEADS = 14
KEY_VALUE_HEADS = 2
HEAD_SIZE = 64
FF = 4864
TOK_DEV = 192
NDOC = 4
STEP = 10
QKVW = 1152
SEQUENCE_COUNT = 4
SEQUENCE_TOKENS = 1536


def draw_doc_lengths(key, part):
    key = jax.random.fold_in(key, 17)
    spare = TOK_DEV // 2
    longest = SEQUENCE_TOKENS - spare

    def one_row(row_key):
        cut_key, place_key = jax.random.split(row_key)
        cuts = jnp.sort(jax.random.permutation(cut_key, spare - 1)[:NDOC - 2] + 1).astype(jnp.int32)
        bounds = jnp.concatenate([jnp.zeros((1,), jnp.int32), cuts, jnp.full((1,), spare, jnp.int32)])
        shorts = bounds[1:] - bounds[:-1]
        chosen = jax.random.randint(place_key, (), 0, NDOC)
        slots = jnp.arange(NDOC, dtype=jnp.int32)
        picked = jnp.clip(slots - (slots > chosen).astype(jnp.int32), 0, NDOC - 2)
        return jnp.where(slots == chosen, longest, shorts[picked]).astype(jnp.int32)
    return jax.vmap(one_row)(jax.random.split(key, SEQUENCE_COUNT))


def spread_log(key, lower, upper):
    unit = jax.random.uniform(key, (QKVW,), jnp.float32)
    return jnp.exp(jnp.log(lower) + unit * (jnp.log(upper) - jnp.log(lower))).astype(jnp.float32)


def draw_second_biases(key, part):
    key = jax.random.fold_in(key, 23)
    token_total = float(SEQUENCE_COUNT * SEQUENCE_TOKENS)
    return spread_log(key, 0.008 * token_total, 0.128 * token_total)


def draw_first_biases(key, part):
    key = jax.random.fold_in(key, 29)
    token_total = float(SEQUENCE_COUNT * SEQUENCE_TOKENS)
    scale = 0.44 * token_total ** 0.5
    return (jax.random.truncated_normal(key, -5.0, 5.0, (QKVW,), jnp.float32) * scale).astype(jnp.float32)


def steps_of(stream_key, dims, shards, low, high):
    def one(dim, blocks):
        steps = jax.random.uniform(jax.random.fold_in(jax.random.fold_in(stream_key, 6), dim), (blocks,), jnp.float32, low / len(shards), high / len(shards))
        return jnp.repeat(jnp.exp(steps), dims[dim] // blocks).reshape((-1,) + (1,) * (len(dims) - dim - 1))

    gain = one(*shards[0])
    for cut in shards[1:]:
        gain = gain * one(*cut)
    return gain


def normal_values(own_key, dims, scale, most, cuts=(), held_as=jnp.bfloat16):
    entries = scale * jax.random.normal(own_key, dims, jnp.float32)
    if cuts:
        entries = entries * steps_of(own_key, dims, cuts, -0.22, 0.18)
    return jnp.clip(entries, -most, most).astype(held_as)


def setup_inputs(seed: int = 0) -> dict:
    streams_of = jax.random.split(jax.random.key(seed), 22)
    return {
        "tokens": normal_values(streams_of[0], (SEQUENCE_COUNT, SEQUENCE_TOKENS, D), 1.0, 6.0, ((0, 4), (1, 8))),
        "cotangent": normal_values(streams_of[1], (SEQUENCE_COUNT, SEQUENCE_TOKENS, D), 1.0, 6.0, ((0, 4), (1, 8))),
        "doc_lengths": draw_doc_lengths(jax.random.fold_in(streams_of[21], 71), 0),
        "w_attn_in": normal_values(streams_of[3], (D, QKVW), D ** -0.5, 0.1875, ((0, 4),), jnp.float32),
        "w_attn_out": normal_values(streams_of[4], (QUERY_HEADS * HEAD_SIZE, D), (max(1, QUERY_HEADS * HEAD_SIZE * 6 // SEQUENCE_TOKENS)) ** -0.5, 3.5, ((0, 4),), jnp.float32),
        "w_mlp_in": normal_values(streams_of[5], (D, 2 * FF), D ** -0.5, 0.1875, ((0, 4),), jnp.float32),
        "w_mlp_out": normal_values(streams_of[6], (FF, D), FF ** -0.5, 0.078125, ((0, 4),), jnp.float32),
        "gains": jnp.clip(1.0 + 0.1 * jax.random.normal(streams_of[7], (2, D), jnp.float32), 0.5, 1.5),
        "biases": normal_values(streams_of[8], (QKVW,), 0.02, 0.12, ((0, 4),), jnp.float32),
        "first_attn_in": normal_values(streams_of[9], (D, QKVW), (0.44 * (SEQUENCE_COUNT * SEQUENCE_TOKENS) ** 0.5), 172.44408, ((0, 4),), jnp.float32),
        "first_attn_out": normal_values(streams_of[10], (QUERY_HEADS * HEAD_SIZE, D), (0.11 * (6 * SEQUENCE_COUNT) ** 0.5), 2.6944387, ((0, 4),), jnp.float32),
        "first_mlp_in": normal_values(streams_of[11], (D, 2 * FF), (0.0275 * (SEQUENCE_COUNT * SEQUENCE_TOKENS) ** 0.5), 10.973714, ((0, 4),), jnp.float32),
        "first_mlp_out": normal_values(streams_of[12], (FF, D), (0.066 * (SEQUENCE_COUNT * SEQUENCE_TOKENS) ** 0.5), 25.866611, ((0, 4),), jnp.float32),
        "first_gains": normal_values(streams_of[13], (2, D), (0.33 * (SEQUENCE_COUNT * SEQUENCE_TOKENS) ** 0.5), 129.33305, ((1, 4),), jnp.float32),
        "first_biases": draw_first_biases(jax.random.fold_in(streams_of[21], 71), 0),
        "second_attn_in": jnp.clip(jnp.exp(math.log(786.432) - 2.7725887 * jax.random.uniform(streams_of[15], (D, QKVW), jnp.float32) ** steps_of(streams_of[15], (D, QKVW), ((0, 4),), -0.2, 0.2)), 49.152, 786.432),
        "second_attn_out": jnp.clip(jnp.exp(math.log(0.192) - 2.7725887 * jax.random.uniform(streams_of[16], (QUERY_HEADS * HEAD_SIZE, D), jnp.float32) ** steps_of(streams_of[16], (QUERY_HEADS * HEAD_SIZE, D), ((0, 4),), -0.2, 0.2)), 0.012, 0.192),
        "second_mlp_in": jnp.clip(jnp.exp(math.log(3.072) - 2.7725887 * jax.random.uniform(streams_of[17], (D, 2 * FF), jnp.float32) ** steps_of(streams_of[17], (D, 2 * FF), ((0, 4),), -0.2, 0.2)), 0.192, 3.072),
        "second_mlp_out": jnp.clip(jnp.exp(math.log(17.69472) - 2.7725887 * jax.random.uniform(streams_of[18], (FF, D), jnp.float32) ** steps_of(streams_of[18], (FF, D), ((0, 4),), -0.2, 0.2)), 1.10592, 17.69472),
        "second_gains": jnp.clip(jnp.exp(math.log(442.368) - 2.7725887 * jax.random.uniform(streams_of[19], (2, D), jnp.float32) ** steps_of(streams_of[19], (2, D), ((1, 4),), -0.2, 0.2)), 27.648, 442.368),
        "second_biases": draw_second_biases(jax.random.fold_in(streams_of[21], 71), 0),
    }


@jax.custom_vjp
def reduced_precision(v):
    return lax.optimization_barrier(v.astype(jnp.bfloat16)).astype(jnp.float32)

@jax.custom_vjp
def reduced_backward(v):
    return v

def low_keep(v):
    return (reduced_precision(v), None)

def low_pass(kept, grad):
    return (grad,)

def back_keep(v):
    return (v, None)

def back_low(kept, grad):
    return (reduced_precision(grad),)
reduced_precision.defvjp(low_keep, low_pass)
reduced_backward.defvjp(back_keep, back_low)
norm_eps = 1e-06
rope_base = 1000000.0
beta_one = 0.9
beta_two = 0.999
adam_eps = 1e-08
highest_precision = lax.Precision.HIGHEST

def rms_norm(values, gain_vec):
    return values * lax.rsqrt(lax.optimization_barrier(jnp.mean(values * values, axis=-1, keepdims=True)) + norm_eps) * gain_vec

def rotate(values, cosine_table, sine_table):
    half_dim = values.shape[-1] // 2
    turned = jnp.concatenate([-values[..., half_dim:], values[..., :half_dim]], axis=-1)
    return values * cosine_table + turned * sine_table

def layout(lengths):
    places = jnp.arange(SEQUENCE_TOKENS, dtype=jnp.int32)
    doc_ends = jnp.cumsum(lengths, axis=-1).astype(jnp.int32)
    doc_starts = doc_ends - lengths
    doc_ids = lax.optimization_barrier(jnp.sum((places[None, :, None] >= doc_ends[:, None, :]).astype(jnp.int32), axis=-1))
    picked = doc_ids[:, :, None] == jnp.arange(NDOC, dtype=jnp.int32)[None, None, :]
    offsets = lax.optimization_barrier(jnp.sum(jnp.where(picked, doc_starts[:, None, :], 0), axis=-1))
    inside = places[None, :] - offsets
    frequency = rope_base ** (-jnp.arange(0, HEAD_SIZE, 2).astype(jnp.float32) / HEAD_SIZE)
    angles = inside.astype(jnp.float32)[..., None] * frequency
    angles = jnp.concatenate([angles, angles], axis=-1)
    return (doc_ids, jnp.cos(angles)[:, :, None, :], jnp.sin(angles)[:, :, None, :])

def attend(query_rows, key_head_rows, value_head_rows, doc_ids):
    block_length = min(512, SEQUENCE_TOKENS)
    group_count = QUERY_HEADS // KEY_VALUE_HEADS
    places = jnp.arange(SEQUENCE_TOKENS, dtype=jnp.int32)
    query_block_rows = query_rows.reshape(SEQUENCE_TOKENS // block_length, block_length, KEY_VALUE_HEADS, group_count, HEAD_SIZE)
    blocks_doc = doc_ids.reshape(SEQUENCE_TOKENS // block_length, block_length)
    blocks_place = places.reshape(SEQUENCE_TOKENS // block_length, block_length)

    def one_block(block_items):
        part_query, part_doc, part_place = block_items
        scores = jnp.einsum('qhgd,khd->hgqk', part_query, key_head_rows, precision=highest_precision)
        scores = reduced_backward(scores * 0.125)
        allowed = (part_doc[:, None] == doc_ids[None, :]) & (places[None, :] <= part_place[:, None])
        scores = jnp.where(allowed, scores, -1e+30)
        top_score = lax.optimization_barrier(jnp.max(scores, axis=-1, keepdims=True))
        weights = jnp.exp(scores - top_score)
        weights = reduced_precision(weights / lax.optimization_barrier(jnp.sum(weights, axis=-1, keepdims=True)))
        mixed = jnp.einsum('hgqk,khd->qhgd', weights, value_head_rows, precision=highest_precision)
        return mixed.reshape(block_length, QUERY_HEADS * HEAD_SIZE)
    attention_result = lax.map(jax.checkpoint(one_block), (query_block_rows, blocks_doc, blocks_place))
    return attention_result.reshape(SEQUENCE_TOKENS, QUERY_HEADS * HEAD_SIZE)

def forward(inputs, attention_input_weight, attention_output_weight, feedforward_input_weight, feedforward_output_weight, gains, biases, doc_ids, cosine_table, sine_table):
    query_width = QUERY_HEADS * HEAD_SIZE
    key_width = KEY_VALUE_HEADS * HEAD_SIZE
    gain_used = reduced_precision(gains)
    applied_bias = reduced_precision(biases)
    normalized_input = reduced_precision(rms_norm(inputs, gain_used[0]))
    mixed_input = reduced_backward(jnp.einsum('tbz,zn->tbn', normalized_input, reduced_precision(attention_input_weight), precision=highest_precision) + applied_bias)
    query_rows = mixed_input[..., :query_width].reshape(SEQUENCE_COUNT, SEQUENCE_TOKENS, QUERY_HEADS, HEAD_SIZE)
    key_head_rows = mixed_input[..., query_width:query_width + key_width].reshape(SEQUENCE_COUNT, SEQUENCE_TOKENS, KEY_VALUE_HEADS, HEAD_SIZE)
    value_head_rows = mixed_input[..., query_width + key_width:].reshape(SEQUENCE_COUNT, SEQUENCE_TOKENS, KEY_VALUE_HEADS, HEAD_SIZE)
    query_rows = reduced_precision(reduced_backward(rotate(query_rows, cosine_table, sine_table)))
    key_head_rows = reduced_precision(reduced_backward(rotate(key_head_rows, cosine_table, sine_table)))
    value_head_rows = reduced_precision(reduced_backward(value_head_rows))
    attention_result = lax.map(lambda seq_items: attend(*seq_items), (query_rows, key_head_rows, value_head_rows, doc_ids))
    attention_result = reduced_precision(reduced_backward(attention_result))
    residual_branch = reduced_backward(jnp.einsum('nqz,zp->nqp', attention_result, reduced_precision(attention_output_weight), precision=highest_precision))
    middle_state = inputs + residual_branch
    second_normalized = reduced_precision(rms_norm(middle_state, gain_used[1]))
    gate_up_product = reduced_backward(jnp.einsum('tye,ev->tyv', second_normalized, reduced_precision(feedforward_input_weight), precision=highest_precision))
    hidden_state = reduced_precision(jax.nn.silu(gate_up_product[..., :FF]) * gate_up_product[..., FF:])
    return middle_state + reduced_backward(jnp.einsum('pcw,wo->pco', hidden_state, reduced_precision(feedforward_output_weight), precision=highest_precision))

def adamw(weight, gradient, first_old, second_old, step_rate, weight_decay):
    first_new = beta_one * first_old + (1.0 - beta_one) * gradient
    second_new = beta_two * second_old + (1.0 - beta_two) * gradient * gradient
    fixed_one = 1.0 - beta_one ** STEP
    fixed_two = 1.0 - beta_two ** STEP
    step_ratio = first_new / fixed_one / (jnp.sqrt(second_new / fixed_two) + adam_eps)
    return (weight - step_rate * (step_ratio + weight_decay * weight), first_new, second_new)

def reference(tokens, cotangent, doc_lengths, w_attn_in, w_attn_out, w_mlp_in, w_mlp_out, gains, biases, first_attn_in, first_attn_out, first_mlp_in, first_mlp_out, first_gains, first_biases, second_attn_in, second_attn_out, second_mlp_in, second_mlp_out, second_gains, second_biases):
    doc_ids, cosine_table, sine_table = layout(doc_lengths)

    def wrapped(inputs, attention_input_weight, attention_output_weight, feedforward_input_weight, feedforward_output_weight, gain_arr, bias_arr):
        return forward(inputs, attention_input_weight, attention_output_weight, feedforward_input_weight, feedforward_output_weight, gain_arr, bias_arr, doc_ids, cosine_table, sine_table)
    output, pullback = jax.vjp(wrapped, tokens.astype(jnp.float32), w_attn_in, w_attn_out, w_mlp_in, w_mlp_out, gains, biases)
    gradients = pullback(cotangent.astype(jnp.float32))
    upd_attn_in = adamw(w_attn_in, gradients[1], first_attn_in, second_attn_in, 0.02, 0.1)
    upd_attn_out = adamw(w_attn_out, gradients[2], first_attn_out, second_attn_out, 0.5, 0.1)
    upd_mlp_in = adamw(w_mlp_in, gradients[3], first_mlp_in, second_mlp_in, 0.02, 0.1)
    upd_mlp_out = adamw(w_mlp_out, gradients[4], first_mlp_out, second_mlp_out, 0.02, 0.1)
    upd_gains = adamw(gains, gradients[5], first_gains, second_gains, 0.4, 0.0)
    upd_biases = adamw(biases, gradients[6], first_biases, second_biases, 0.02, 0.0)
    return (output.astype(jnp.bfloat16), gradients[0], upd_attn_in[0], upd_attn_in[1], upd_attn_in[2], upd_attn_out[0], upd_attn_out[1], upd_attn_out[2], upd_mlp_in[0], upd_mlp_in[1], upd_mlp_in[2], upd_mlp_out[0], upd_mlp_out[1], upd_mlp_out[2], upd_gains[0], upd_gains[1], upd_gains[2], upd_biases[0], upd_biases[1], upd_biases[2])
```

```python
import jax
import jax.numpy as jnp
from jax import lax
from jax.sharding import PartitionSpec as P

QUERY_HEADS = 14
KEY_VALUE_HEADS = 2
HEAD_SIZE = 64
FF = 4864
NDOC = 4
STEP = 10


norm_eps = 1e-06
rope_base = 1000000.0
beta_one = 0.9
beta_two = 0.999
adam_eps = 1e-08


def rms_parts(values):
    factor = lax.rsqrt(jnp.mean(values * values, axis=-1, keepdims=True) + norm_eps)
    return (values * factor, factor)


def norm_back(incoming, scaled, factor, gain_vec):
    weighted = incoming * gain_vec
    inner = jnp.mean(weighted * scaled, axis=-1, keepdims=True)
    return (factor * (weighted - scaled * inner), jnp.sum(incoming * scaled, axis=0))


def rotate(values, cosine_table, sine_table):
    half_dim = values.shape[-1] // 2
    turned = jnp.concatenate([-values[..., half_dim:], values[..., :half_dim]], axis=-1)
    return values * cosine_table + turned * sine_table


def unrotate(values, cosine_table, sine_table):
    half_dim = values.shape[-1] // 2
    shifted = values * sine_table
    turned = jnp.concatenate([shifted[..., half_dim:], -shifted[..., :half_dim]], axis=-1)
    return values * cosine_table + turned


def times_transposed(left, right):
    return lax.dot_general(
        left, right, (((1,), (1,)), ((), ())), preferred_element_type=jnp.float32
    )


def transposed_times(left, right):
    return lax.dot_general(
        left, right, (((0,), (0,)), ((), ())), preferred_element_type=jnp.float32
    )


def adamw(weight, gradient, first_old, second_old, step_rate, weight_decay):
    first_new = beta_one * first_old + (1.0 - beta_one) * gradient
    second_new = beta_two * second_old + (1.0 - beta_two) * gradient * gradient
    fixed_one = 1.0 - beta_one**STEP
    fixed_two = 1.0 - beta_two**STEP
    step_ratio = first_new / fixed_one / (jnp.sqrt(second_new / fixed_two) + adam_eps)
    return (weight - step_rate * (step_ratio + weight_decay * weight), first_new, second_new)


def over_blocks(count, step, carry):
    if count == 1:
        return step(0, carry)
    return lax.fori_loop(0, count, step, carry)


INNER = 8
CHIPS = 4


def pick(stacked, index):
    return lax.dynamic_index_in_dim(stacked, index, 0, keepdims=False)


def shift_core(values, count):
    return lax.ppermute(values, "ctx", [(i, i ^ 1) for i in range(count)])


def swap_chips(stacked, chip, count):
    received = [
        lax.ppermute(pick(stacked, chip ^ d), "ctx", [(i, i ^ (2 * d)) for i in range(count)])
        for d in range(1, CHIPS)
    ]
    return [pick(stacked, chip)] + received


def swap_fsdp(stacked, place, count):
    received = [
        lax.ppermute(pick(stacked, place ^ d), "fsdp", [(i, i ^ d) for i in range(count)])
        for d in range(1, count)
    ]
    return [pick(stacked, place)] + received


def by_source(entries, place):
    stacked = jnp.stack(entries)
    return jnp.stack([pick(stacked, place ^ j) for j in range(len(entries))])


def total_of(entries):
    out = entries[0].astype(jnp.float32)
    for entry in entries[1:]:
        out = out + entry.astype(jnp.float32)
    return out


def inner_groups(count):
    if count == INNER:
        return None
    return [[g * INNER + i for i in range(INNER)] for g in range(count // INNER)]


def outer_sum(values, count):
    if count == INNER:
        return values
    span = INNER
    while span < count:
        values = values + lax.ppermute(
            values.astype(jnp.bfloat16), "ctx", [(i, i ^ span) for i in range(count)]
        ).astype(jnp.float32)
        span *= 2
    return values


def sum_pair(first_half, second_half, core, count):
    mine = jnp.where(core == 0, first_half, second_half)
    other = jnp.where(core == 0, second_half, first_half)
    arrived = shift_core(other, count)
    return (mine.astype(jnp.float32) + arrived.astype(jnp.float32)).astype(jnp.bfloat16)


def sum_rows(first_half, second_half, core, chip, place, ctx_count, fsdp_count, joined):
    kept = sum_pair(first_half, second_half, core, ctx_count)
    rows, width = kept.shape
    part = rows // (fsdp_count * CHIPS)
    kept = kept.reshape(fsdp_count, CHIPS, part, width).transpose(1, 0, 2, 3)
    chunk = outer_sum(total_of(swap_chips(kept, chip, ctx_count)), ctx_count).astype(jnp.bfloat16)
    pieces = swap_fsdp(chunk, place, fsdp_count)
    if joined:
        owned = by_source(pieces, place)
    else:
        owned = total_of(pieces).astype(jnp.bfloat16)[None]
    full = lax.all_gather(owned, "ctx", axis=0, axis_index_groups=inner_groups(ctx_count))
    slices = owned.shape[0]
    full = full.reshape(CHIPS, 2, slices, part, width).transpose(0, 3, 1, 2, 4)
    return full.reshape(CHIPS * part, 2 * slices * width).astype(jnp.float32)


def body(
    tokens,
    cotangent,
    doc_lengths,
    w_attn_in,
    w_attn_out,
    w_mlp_in,
    w_mlp_out,
    gains,
    biases,
    first_attn_in,
    first_attn_out,
    first_mlp_in,
    first_mlp_out,
    first_gains,
    first_biases,
    second_attn_in,
    second_attn_out,
    second_mlp_in,
    second_mlp_out,
    second_gains,
    second_biases,
):
    token_rows = tokens.shape[1]
    ctx_count = lax.axis_size("ctx")
    ctx_index = lax.axis_index("ctx")
    seq_len = token_rows * ctx_count
    current_key_block = min(1536, seq_len)
    number_of_blocks = seq_len // current_key_block
    group_count = QUERY_HEADS // KEY_VALUE_HEADS
    query_width = QUERY_HEADS * HEAD_SIZE
    key_width = KEY_VALUE_HEADS * HEAD_SIZE
    inputs = tokens[0].astype(jnp.float32)
    upstream = cotangent[0]
    lengths_row = doc_lengths[0]
    doc_ends = jnp.cumsum(lengths_row)
    doc_starts = doc_ends - lengths_row
    key_place = jnp.arange(seq_len, dtype=jnp.int32)
    key_doc = jnp.sum((key_place[:, None] >= doc_ends[None, :]).astype(jnp.int32), axis=1)
    query_place = ctx_index * token_rows + jnp.arange(token_rows, dtype=jnp.int32)
    query_doc = lax.dynamic_slice_in_dim(key_doc, ctx_index * token_rows, token_rows)
    picked = query_doc[:, None] == jnp.arange(NDOC, dtype=jnp.int32)[None, :]
    inside = query_place - jnp.sum(jnp.where(picked, doc_starts[None, :], 0), axis=1)
    frequency = rope_base ** (-jnp.arange(0, HEAD_SIZE, 2).astype(jnp.float32) / HEAD_SIZE)
    angles = inside.astype(jnp.float32)[:, None] * frequency[None, :]
    angles = jnp.concatenate([angles, angles], axis=-1)
    cosine_table = jnp.cos(angles)[:, None, :]
    sine_table = jnp.sin(angles)[:, None, :]
    last_place = ctx_index * token_rows + token_rows - 1
    fsdp_count = lax.axis_size("fsdp")
    place = lax.axis_index("fsdp")
    core = lax.rem(ctx_index, 2)
    inner = lax.rem(ctx_index, INNER)
    chip = inner // 2
    groups = inner_groups(ctx_count)
    slice_rows = w_mlp_out.shape[0]
    shard_rows = w_attn_in.shape[0]
    in_width = w_attn_in.shape[1]
    part_rows = shard_rows // INNER
    small = jnp.concatenate([gains[0], gains[1], biases]).astype(jnp.bfloat16)
    small = jnp.pad(small, (0, in_width - small.shape[0]))
    own_part = lax.dynamic_slice_in_dim(w_attn_in, inner * part_rows, part_rows, 0)
    packed = jnp.concatenate([own_part.astype(jnp.bfloat16), small[None]], axis=0)
    packed = jnp.pad(packed, ((0, 32 - packed.shape[0]), (0, 0)))
    packed = lax.all_gather(packed, "fsdp", axis=0)
    packed = lax.all_gather(packed, "ctx", axis=0, axis_index_groups=groups)
    attn_in_low = packed[:, :, :part_rows].transpose(1, 0, 2, 3).reshape(-1, in_width)
    small_all = packed[0, :, part_rows]
    gains_low = small_all[:, : 2 * shard_rows].reshape(fsdp_count, 2, shard_rows)
    gains_low = gains_low.transpose(1, 0, 2).reshape(2, -1)
    bias_end = 2 * shard_rows + biases.shape[0]
    biases_low = small_all[:, 2 * shard_rows : bias_end].reshape(-1)
    out_part = lax.dynamic_slice_in_dim(w_attn_out, inner * part_rows, part_rows, 0)
    out_part = lax.all_gather(out_part.astype(jnp.bfloat16), "fsdp", axis=0)
    out_part = lax.all_gather(out_part, "ctx", axis=0, axis_index_groups=groups)
    attn_out_low = out_part.transpose(1, 0, 2, 3).reshape(-1, w_attn_out.shape[1])
    mlp_out_low = w_mlp_out.astype(jnp.bfloat16)
    own_kind = lax.dynamic_slice_in_dim(w_mlp_in, core * FF, FF, 1).astype(jnp.bfloat16)
    own_kind = own_kind.reshape(shard_rows, fsdp_count, slice_rows).transpose(1, 0, 2)
    own_kind = by_source(swap_fsdp(own_kind, place, fsdp_count), place).reshape(-1, slice_rows)
    other_kind = shift_core(own_kind, ctx_count)
    gate_low = jnp.where(core == 0, own_kind, other_kind)
    up_low = jnp.where(core == 0, other_kind, own_kind)
    upstream_all = lax.all_gather(upstream, "fsdp", axis=0, tiled=True)
    gain_one = gains_low[0].astype(jnp.float32)
    gain_two = gains_low[1].astype(jnp.float32)
    scaled_one, factor_one = rms_parts(inputs)
    normed_one = (scaled_one * gain_one).astype(jnp.bfloat16)
    mixed_input = jnp.dot(
        normed_one, attn_in_low, preferred_element_type=jnp.float32
    ) + biases_low.astype(jnp.float32)
    query_rows = rotate(
        mixed_input[:, :query_width].reshape(token_rows, QUERY_HEADS, HEAD_SIZE),
        cosine_table,
        sine_table,
    ).astype(jnp.bfloat16)
    key_head_rows = rotate(
        mixed_input[:, query_width : query_width + key_width].reshape(
            token_rows, KEY_VALUE_HEADS, HEAD_SIZE
        ),
        cosine_table,
        sine_table,
    )
    key_head_rows = key_head_rows.astype(jnp.bfloat16).reshape(token_rows, key_width)
    value_head_rows = mixed_input[:, query_width + key_width :].astype(jnp.bfloat16)
    joined_rows = lax.all_gather(
        jnp.concatenate([key_head_rows, value_head_rows], axis=1), "ctx", axis=0, tiled=True
    )
    all_keys = joined_rows[:, :key_width]
    all_values = joined_rows[:, key_width:]
    grouped_queries = query_rows.reshape(token_rows, KEY_VALUE_HEADS, group_count, HEAD_SIZE)

    def block_data(source_keys, values_src, block_index):
        block_offset = block_index * current_key_block
        key_row_matrix = lax.dynamic_slice_in_dim(
            source_keys, block_offset, current_key_block
        ).reshape(current_key_block, KEY_VALUE_HEADS, HEAD_SIZE)
        value_rows = lax.dynamic_slice_in_dim(values_src, block_offset, current_key_block).reshape(
            current_key_block, KEY_VALUE_HEADS, HEAD_SIZE
        )
        doc_slice = lax.dynamic_slice_in_dim(key_doc, block_offset, current_key_block)
        place_slice = lax.dynamic_slice_in_dim(key_place, block_offset, current_key_block)
        scores = (
            jnp.einsum(
                "qhgd,khd->hgqk",
                grouped_queries,
                key_row_matrix,
                preferred_element_type=jnp.float32,
            )
            * 0.125
        )
        allowed = (query_doc[:, None] == doc_slice[None, :]) & (
            place_slice[None, :] <= query_place[:, None]
        )
        return (key_row_matrix, value_rows, scores, allowed)

    def lse_step(block_index, carry):

        def lse_active(state):
            running_max, running_sum = state
            key_row_matrix, value_rows, scores, allowed = block_data(
                all_keys, all_values, block_index
            )
            masked = jnp.where(allowed, scores, -1e30)
            new_max = jnp.maximum(running_max, jnp.max(masked, axis=-1))
            terms = jnp.where(allowed, jnp.exp(masked - new_max[..., None]), 0.0)
            return (new_max, running_sum * jnp.exp(running_max - new_max) + jnp.sum(terms, axis=-1))

        if number_of_blocks == 1:
            return lse_active(carry)
        return lax.cond(
            block_index * current_key_block <= last_place, lse_active, lambda state: state, carry
        )

    initial_maximum = jnp.full((KEY_VALUE_HEADS, group_count, token_rows), -1e30, jnp.float32)
    initial_sum = jnp.zeros((KEY_VALUE_HEADS, group_count, token_rows), jnp.float32)
    final_max, final_sum = over_blocks(
        number_of_blocks, lse_step, (initial_maximum, initial_sum)
    )
    log_total = final_max + jnp.log(final_sum)

    def output_update(block_index, carry):

        def output_active(accum):
            key_row_matrix, value_rows, scores, allowed = block_data(
                all_keys, all_values, block_index
            )
            probs = jnp.where(allowed, jnp.exp(scores - log_total[..., None]), 0.0).astype(
                jnp.bfloat16
            )
            return accum + jnp.einsum(
                "hgqk,khd->qhgd", probs, value_rows, preferred_element_type=jnp.float32
            )

        if number_of_blocks == 1:
            return output_active(carry)
        return lax.cond(
            block_index * current_key_block <= last_place, output_active, lambda accum: accum, carry
        )

    attention_result = over_blocks(
        number_of_blocks,
        output_update,
        jnp.zeros((token_rows, KEY_VALUE_HEADS, group_count, HEAD_SIZE), jnp.float32),
    )
    attended_low = attention_result.reshape(token_rows, query_width).astype(jnp.bfloat16)
    middle_state = inputs + jnp.dot(attended_low, attn_out_low, preferred_element_type=jnp.float32)
    scaled_two, factor_two = rms_parts(middle_state)
    second_normalized = (scaled_two * gain_two).astype(jnp.bfloat16)
    second_all = lax.all_gather(second_normalized, "fsdp", axis=0, tiled=True)
    gate_val = jnp.dot(second_all, gate_low, preferred_element_type=jnp.float32)
    up_val = jnp.dot(second_all, up_low, preferred_element_type=jnp.float32)
    sigmoid_val = jax.nn.sigmoid(gate_val)
    silu_val = gate_val * sigmoid_val
    hidden_state = (silu_val * up_val).astype(jnp.bfloat16)
    hidden_grad = times_transposed(upstream_all, mlp_out_low)
    silu_slope = sigmoid_val * (1.0 + gate_val * (1.0 - sigmoid_val))
    gate_grad = (hidden_grad * up_val * silu_slope).astype(jnp.bfloat16)
    up_grad = (hidden_grad * silu_val).astype(jnp.bfloat16)
    normed_two_part = times_transposed(gate_grad, gate_low) + times_transposed(up_grad, up_low)
    normed_two_part = normed_two_part.astype(jnp.bfloat16).reshape(fsdp_count, token_rows, -1)
    normed_two_grad = total_of(swap_fsdp(normed_two_part, place, fsdp_count))
    output_part = jnp.dot(hidden_state, mlp_out_low, preferred_element_type=jnp.float32)
    output_part = output_part.astype(jnp.bfloat16).reshape(fsdp_count, token_rows, -1)
    output = middle_state + total_of(swap_fsdp(output_part, place, fsdp_count))
    mlp_in_grad = sum_rows(
        transposed_times(second_all, gate_grad).astype(jnp.bfloat16),
        transposed_times(second_all, up_grad).astype(jnp.bfloat16),
        core, chip, place, ctx_count, fsdp_count, True,
    )
    mlp_out_part = transposed_times(hidden_state, upstream_all).astype(jnp.bfloat16)
    mlp_out_part = mlp_out_part.reshape(CHIPS, 2, -1, mlp_out_part.shape[1])
    mlp_out_part = sum_pair(mlp_out_part[:, 0], mlp_out_part[:, 1], core, ctx_count)
    mlp_out_part = outer_sum(total_of(swap_chips(mlp_out_part, chip, ctx_count)), ctx_count)
    mlp_out_grad = lax.all_gather(
        mlp_out_part.astype(jnp.bfloat16), "ctx", axis=0, axis_index_groups=groups, tiled=True
    ).astype(jnp.float32)
    middle_norm_grad, gain_two_grad = norm_back(
        normed_two_grad, scaled_two, factor_two, gain_two
    )
    middle_grad = upstream.astype(jnp.float32) + middle_norm_grad
    branch_grad = middle_grad.astype(jnp.bfloat16)
    head_gradient = times_transposed(branch_grad, attn_out_low).astype(jnp.bfloat16)
    grouped_head_gradient = head_gradient.reshape(
        token_rows, KEY_VALUE_HEADS, group_count, HEAD_SIZE
    )
    delta = jnp.einsum(
        "qhgd,qhgd->hgq", grouped_head_gradient.astype(jnp.float32), attention_result
    )
    attn_out_part = transposed_times(attended_low, branch_grad).astype(jnp.bfloat16)
    out_half = attn_out_part.shape[1] // 2
    attn_out_grad = sum_rows(
        attn_out_part[:, :out_half], attn_out_part[:, out_half:],
        core, chip, place, ctx_count, fsdp_count, False,
    )

    def back_step(block_index, carry):

        def back_active(state):
            query_grad, key_grad, value_grad = state
            key_row_matrix, value_rows, scores, allowed = block_data(
                all_keys, all_values, block_index
            )
            probs = jnp.where(allowed, jnp.exp(scores - log_total[..., None]), 0.0)
            probs_low = probs.astype(jnp.bfloat16)
            prob_grad = jnp.einsum(
                "qhgd,khd->hgqk",
                grouped_head_gradient,
                value_rows,
                preferred_element_type=jnp.float32,
            )
            score_grad = (probs * (prob_grad - delta[..., None])).astype(jnp.bfloat16)
            query_grad = (
                query_grad
                + jnp.einsum(
                    "hgqk,khd->qhgd", score_grad, key_row_matrix, preferred_element_type=jnp.float32
                )
                * 0.125
            )
            key_part = (
                jnp.einsum(
                    "hgqk,qhgd->khd",
                    score_grad,
                    grouped_queries,
                    preferred_element_type=jnp.float32,
                )
                * 0.125
            )
            value_part = jnp.einsum(
                "hgqk,qhgd->khd",
                probs_low,
                grouped_head_gradient,
                preferred_element_type=jnp.float32,
            )
            block_offset = block_index * current_key_block
            key_grad = lax.dynamic_update_slice_in_dim(
                key_grad, key_part.reshape(current_key_block, key_width), block_offset, 0
            )
            value_grad = lax.dynamic_update_slice_in_dim(
                value_grad, value_part.reshape(current_key_block, key_width), block_offset, 0
            )
            return (query_grad, key_grad, value_grad)

        if number_of_blocks == 1:
            return back_active(carry)
        return lax.cond(
            block_index * current_key_block <= last_place, back_active, lambda state: state, carry
        )

    start_state = (
        jnp.zeros((token_rows, KEY_VALUE_HEADS, group_count, HEAD_SIZE), jnp.float32),
        jnp.zeros((seq_len, key_width), jnp.float32),
        jnp.zeros((seq_len, key_width), jnp.float32),
    )
    query_grad, key_grad, value_grad = over_blocks(number_of_blocks, back_step, start_state)
    pair_grad = jnp.concatenate([key_grad, value_grad], axis=1)
    if ctx_count == INNER:
        pair_grad = pair_grad.astype(jnp.bfloat16).reshape(CHIPS, 2, token_rows, 2 * key_width)
        pair_grad = sum_pair(pair_grad[:, 0], pair_grad[:, 1], core, ctx_count)
        pair_sum = total_of(swap_chips(pair_grad, chip, ctx_count))
    else:
        pair_sum = lax.psum_scatter(pair_grad, "ctx", scatter_dimension=0, tiled=True)
    key_total_sum = pair_sum[:, :key_width]
    value_sum = pair_sum[:, key_width:]
    query_low = (
        query_grad.astype(jnp.bfloat16)
        .astype(jnp.float32)
        .reshape(token_rows, QUERY_HEADS, HEAD_SIZE)
    )
    key_reduced = (
        key_total_sum.astype(jnp.bfloat16)
        .astype(jnp.float32)
        .reshape(token_rows, KEY_VALUE_HEADS, HEAD_SIZE)
    )
    value_low = value_sum.astype(jnp.bfloat16).astype(jnp.float32)
    pre_grad = jnp.concatenate(
        [
            unrotate(query_low, cosine_table, sine_table).reshape(token_rows, query_width),
            unrotate(key_reduced, cosine_table, sine_table).reshape(token_rows, key_width),
            value_low,
        ],
        axis=1,
    ).astype(jnp.bfloat16)
    bias_grad = jnp.sum(pre_grad.astype(jnp.float32), axis=0)
    normed_one_grad = times_transposed(pre_grad, attn_in_low)
    input_norm_grad, gain_one_grad = norm_back(
        normed_one_grad, scaled_one, factor_one, gain_one
    )
    input_grad = middle_grad + input_norm_grad
    attn_in_part = transposed_times(normed_one, pre_grad).astype(jnp.bfloat16)
    in_half = in_width // 2
    attn_in_grad = sum_rows(
        attn_in_part[:, :in_half], attn_in_part[:, in_half:],
        core, chip, place, ctx_count, fsdp_count, False,
    )
    vectors = lax.psum(
        jnp.concatenate([gain_one_grad, gain_two_grad, bias_grad]), ("ctx", "fsdp")
    )
    model_width = gain_one_grad.shape[0]
    gains_grad = lax.dynamic_slice_in_dim(
        vectors[: 2 * model_width].reshape(2, model_width), place * shard_rows, shard_rows, 1
    )
    biases_grad = lax.dynamic_slice_in_dim(
        vectors[2 * model_width :], place * biases.shape[0], biases.shape[0], 0
    )
    totals = (
        attn_in_grad, attn_out_grad, mlp_in_grad, mlp_out_grad, gains_grad, biases_grad,
    )
    upd_attn_in = adamw(w_attn_in, totals[0], first_attn_in, second_attn_in, 0.02, 0.1)
    upd_attn_out = adamw(w_attn_out, totals[1], first_attn_out, second_attn_out, 0.5, 0.1)
    upd_mlp_in = adamw(w_mlp_in, totals[2], first_mlp_in, second_mlp_in, 0.02, 0.1)
    upd_mlp_out = adamw(w_mlp_out, totals[3], first_mlp_out, second_mlp_out, 0.02, 0.1)
    upd_gains = adamw(gains, totals[4], first_gains, second_gains, 0.4, 0.0)
    upd_biases = adamw(biases, totals[5], first_biases, second_biases, 0.02, 0.0)
    return (
        output.astype(jnp.bfloat16)[None],
        input_grad[None],
        upd_attn_in[0],
        upd_attn_in[1],
        upd_attn_in[2],
        upd_attn_out[0],
        upd_attn_out[1],
        upd_attn_out[2],
        upd_mlp_in[0],
        upd_mlp_in[1],
        upd_mlp_in[2],
        upd_mlp_out[0],
        upd_mlp_out[1],
        upd_mlp_out[2],
        upd_gains[0],
        upd_gains[1],
        upd_gains[2],
        upd_biases[0],
        upd_biases[1],
        upd_biases[2],
    )


def solution(mesh):
    return jax.shard_map(
        body,
        mesh=mesh,
        in_specs=(
            P("fsdp", "ctx", None),
            P("fsdp", "ctx", None),
            P("fsdp", None),
            P("fsdp", None),
            P("fsdp", None),
            P("fsdp", None),
            P("fsdp", None),
            P(None, "fsdp"),
            P("fsdp"),
            P("fsdp", None),
            P("fsdp", None),
            P("fsdp", None),
            P("fsdp", None),
            P(None, "fsdp"),
            P("fsdp"),
            P("fsdp", None),
            P("fsdp", None),
            P("fsdp", None),
            P("fsdp", None),
            P(None, "fsdp"),
            P("fsdp"),
        ),
        out_specs=(
            P("fsdp", "ctx", None),
            P("fsdp", "ctx", None),
            P("fsdp", None),
            P("fsdp", None),
            P("fsdp", None),
            P("fsdp", None),
            P("fsdp", None),
            P("fsdp", None),
            P("fsdp", None),
            P("fsdp", None),
            P("fsdp", None),
            P("fsdp", None),
            P("fsdp", None),
            P("fsdp", None),
            P(None, "fsdp"),
            P(None, "fsdp"),
            P(None, "fsdp"),
            P("fsdp"),
            P("fsdp"),
            P("fsdp"),
        ),
        check_vma=False,
    )
```

```python
import jax
import jax.numpy as jnp
from jax import lax
from jax.experimental import pallas as pl
from jax.experimental.pallas import tpu as pltpu
from jax.sharding import PartitionSpec as P

QUERY_HEADS = 14
KEY_VALUE_HEADS = 2
HEAD_SIZE = 64
FF = 4864
NDOC = 4
STEP = 10


norm_eps = 1e-06
rope_base = 1000000.0
beta_one = 0.9
beta_two = 0.999
adam_eps = 1e-08


def rms_parts(values):
    factor = lax.rsqrt(jnp.mean(values * values, axis=-1, keepdims=True) + norm_eps)
    return (values * factor, factor)


def norm_back(incoming, scaled, factor, gain_vec):
    weighted = incoming * gain_vec
    inner = jnp.mean(weighted * scaled, axis=-1, keepdims=True)
    return (factor * (weighted - scaled * inner), jnp.sum(incoming * scaled, axis=0))


def rotate(values, cosine_table, sine_table):
    half_dim = values.shape[-1] // 2
    turned = jnp.concatenate([-values[..., half_dim:], values[..., :half_dim]], axis=-1)
    return values * cosine_table + turned * sine_table


def unrotate(values, cosine_table, sine_table):
    half_dim = values.shape[-1] // 2
    shifted = values * sine_table
    turned = jnp.concatenate([shifted[..., half_dim:], -shifted[..., :half_dim]], axis=-1)
    return values * cosine_table + turned


def times_transposed(left, right):
    return lax.dot_general(
        left, right, (((1,), (1,)), ((), ())), preferred_element_type=jnp.float32
    )


def transposed_times(left, right):
    return lax.dot_general(
        left, right, (((0,), (0,)), ((), ())), preferred_element_type=jnp.float32
    )


def adamw(weight, gradient, first_old, second_old, step_rate, weight_decay):
    first_new = beta_one * first_old + (1.0 - beta_one) * gradient
    second_new = beta_two * second_old + (1.0 - beta_two) * gradient * gradient
    fixed_one = 1.0 - beta_one**STEP
    fixed_two = 1.0 - beta_two**STEP
    step_ratio = first_new / fixed_one / (jnp.sqrt(second_new / fixed_two) + adam_eps)
    return (weight - step_rate * (step_ratio + weight_decay * weight), first_new, second_new)


def over_blocks(count, step, carry):
    if count == 1:
        return step(0, carry)
    return lax.fori_loop(0, count, step, carry)


INNER = 8
CHIPS = 4


def pick(stacked, index):
    return lax.dynamic_index_in_dim(stacked, index, 0, keepdims=False)


def shift_core(values, count):
    return lax.ppermute(values, "ctx", [(i, i ^ 1) for i in range(count)])


def send_chips(stacked, chip, count):
    received = [
        lax.ppermute(pick(stacked, chip ^ d), "ctx", [(i, i ^ (2 * d)) for i in range(count)])
        for d in range(1, CHIPS)
    ]
    return [pick(stacked, chip)] + received


def send_fsdp(stacked, place, count):
    received = [
        lax.ppermute(pick(stacked, place ^ d), "fsdp", [(i, i ^ d) for i in range(count)])
        for d in range(1, count)
    ]
    return [pick(stacked, place)] + received


def share_fsdp(values, count):
    received = [
        lax.ppermute(values, "fsdp", [(i, i ^ d) for i in range(count)]) for d in range(1, count)
    ]
    return [values] + received


def return_fsdp(blocks, count):
    received = [
        lax.ppermute(blocks[d], "fsdp", [(i, i ^ d) for i in range(count)])
        for d in range(1, count)
    ]
    return [blocks[0]] + received


def tie(*values):
    return lax.optimization_barrier(values)


def by_source(entries, place):
    stacked = jnp.stack(entries)
    return jnp.stack([pick(stacked, place ^ j) for j in range(len(entries))])


def total_of(entries):
    out = entries[0].astype(jnp.float32)
    for entry in entries[1:]:
        out = out + entry.astype(jnp.float32)
    return out


def inner_groups(count):
    if count == INNER:
        return None
    return [[g * INNER + i for i in range(INNER)] for g in range(count // INNER)]


def outer_sum(values, count):
    if count == INNER:
        return values
    span = INNER
    while span < count:
        values = values + lax.ppermute(
            values.astype(jnp.bfloat16), "ctx", [(i, i ^ span) for i in range(count)]
        ).astype(jnp.float32)
        span *= 2
    return values


def sum_pair(first_half, second_half, core, count):
    mine = jnp.where(core == 0, first_half, second_half)
    other = jnp.where(core == 0, second_half, first_half)
    arrived = shift_core(other, count)
    return (mine.astype(jnp.float32) + arrived.astype(jnp.float32)).astype(jnp.bfloat16)


def by_chip(kept, fsdp_count):
    rows, width = kept.shape
    part = rows // (fsdp_count * CHIPS)
    return kept.reshape(fsdp_count, CHIPS, part, width).transpose(1, 0, 2, 3)


def adamw_kernel(w_ref, g_ref, first_ref, second_ref, w_out, first_out, second_out):
    slices, width = g_ref.shape[2], g_ref.shape[4]
    for j in range(slices):
        span = slice(j * width, (j + 1) * width)
        new, first_new, second_new = adamw(
            w_ref[:, span],
            g_ref[0, 0, j].astype(jnp.float32),
            first_ref[:, span],
            second_ref[:, span],
            0.02,
            0.1,
        )
        w_out[:, span] = new
        first_out[:, span] = first_new
        second_out[:, span] = second_new


def adamw_blocks(weight, blocks, first_old, second_old):
    chips, kinds, slices, part, width = blocks.shape
    whole = pl.BlockSpec((part, slices * width), lambda i, k: (i, k))
    piece = pl.BlockSpec((1, 1, slices, part, width), lambda i, k: (i, k, 0, 0, 0))
    shape = jax.ShapeDtypeStruct(weight.shape, jnp.float32)
    return pl.pallas_call(
        adamw_kernel,
        grid=(chips, kinds),
        in_specs=[whole, piece, whole, whole],
        out_specs=[whole, whole, whole],
        out_shape=[shape, shape, shape],
        compiler_params=pltpu.CompilerParams(vmem_limit_bytes=40 * 2**20),
        cost_estimate=pl.CostEstimate(
            flops=14 * weight.size, bytes_accessed=26 * weight.size, transcendentals=weight.size
        ),
    )(weight, blocks, first_old, second_old)


def body(
    tokens,
    cotangent,
    doc_lengths,
    w_attn_in,
    w_attn_out,
    w_mlp_in,
    w_mlp_out,
    gains,
    biases,
    first_attn_in,
    first_attn_out,
    first_mlp_in,
    first_mlp_out,
    first_gains,
    first_biases,
    second_attn_in,
    second_attn_out,
    second_mlp_in,
    second_mlp_out,
    second_gains,
    second_biases,
):
    token_rows = tokens.shape[1]
    ctx_count = lax.axis_size("ctx")
    ctx_index = lax.axis_index("ctx")
    seq_len = token_rows * ctx_count
    current_key_block = min(1536, seq_len)
    number_of_blocks = seq_len // current_key_block
    group_count = QUERY_HEADS // KEY_VALUE_HEADS
    query_width = QUERY_HEADS * HEAD_SIZE
    key_width = KEY_VALUE_HEADS * HEAD_SIZE
    inputs = tokens[0].astype(jnp.float32)
    upstream = cotangent[0]
    lengths_row = doc_lengths[0]
    doc_ends = jnp.cumsum(lengths_row)
    doc_starts = doc_ends - lengths_row
    key_place = jnp.arange(seq_len, dtype=jnp.int32)
    key_doc = jnp.sum((key_place[:, None] >= doc_ends[None, :]).astype(jnp.int32), axis=1)
    query_place = ctx_index * token_rows + jnp.arange(token_rows, dtype=jnp.int32)
    query_doc = lax.dynamic_slice_in_dim(key_doc, ctx_index * token_rows, token_rows)
    picked = query_doc[:, None] == jnp.arange(NDOC, dtype=jnp.int32)[None, :]
    inside = query_place - jnp.sum(jnp.where(picked, doc_starts[None, :], 0), axis=1)
    frequency = rope_base ** (-jnp.arange(0, HEAD_SIZE, 2).astype(jnp.float32) / HEAD_SIZE)
    angles = inside.astype(jnp.float32)[:, None] * frequency[None, :]
    angles = jnp.concatenate([angles, angles], axis=-1)
    cosine_table = jnp.cos(angles)[:, None, :]
    sine_table = jnp.sin(angles)[:, None, :]
    last_place = ctx_index * token_rows + token_rows - 1
    fsdp_count = lax.axis_size("fsdp")
    place = lax.axis_index("fsdp")
    core = lax.rem(ctx_index, 2)
    inner = lax.rem(ctx_index, INNER)
    chip = inner // 2
    groups = inner_groups(ctx_count)
    slice_rows = w_mlp_out.shape[0]
    shard_rows = w_attn_in.shape[0]
    in_width = w_attn_in.shape[1]
    part_rows = shard_rows // INNER
    small = jnp.concatenate([gains[0], gains[1], biases]).astype(jnp.bfloat16)
    width = in_width + w_attn_out.shape[1]
    attn_weights = jnp.concatenate([w_attn_in, w_attn_out], axis=1)
    own_part = lax.dynamic_slice_in_dim(attn_weights, inner * part_rows, part_rows, 0)
    small = jnp.pad(small, (0, width - small.shape[0]))
    packed = jnp.concatenate([own_part.astype(jnp.bfloat16), small[None]], axis=0)
    packed = jnp.pad(packed, ((0, 32 - packed.shape[0]), (0, 0)))
    if ctx_count == INNER:
        packed = lax.all_gather(packed, ("ctx", "fsdp"), axis=0)
        packed = packed.reshape(INNER, fsdp_count, 32, width)
    else:
        packed = lax.all_gather(packed, "fsdp", axis=0)
        packed = lax.all_gather(packed, "ctx", axis=0, axis_index_groups=groups)
    attn_low = packed[:, :, :part_rows].transpose(1, 0, 2, 3).reshape(-1, width)
    attn_in_low = attn_low[:, :in_width]
    attn_out_low = attn_low[:, in_width:]
    small_all = packed[0, :, part_rows]
    gains_low = small_all[:, : 2 * shard_rows].reshape(fsdp_count, 2, shard_rows)
    gains_low = gains_low.transpose(1, 0, 2).reshape(2, -1)
    bias_end = 2 * shard_rows + biases.shape[0]
    biases_low = small_all[:, 2 * shard_rows : bias_end].reshape(-1)
    mlp_out_low = w_mlp_out.astype(jnp.bfloat16)
    own_kind = lax.dynamic_slice_in_dim(w_mlp_in, core * FF, FF, 1).astype(jnp.bfloat16)
    own_kind = own_kind.reshape(shard_rows, fsdp_count, slice_rows).transpose(1, 0, 2)
    own_kinds = send_fsdp(own_kind, place, fsdp_count)
    upstream_parts = share_fsdp(upstream, fsdp_count)
    gain_one = gains_low[0].astype(jnp.float32)
    gain_two = gains_low[1].astype(jnp.float32)
    scaled_one, factor_one = rms_parts(inputs)
    normed_one = (scaled_one * gain_one).astype(jnp.bfloat16)
    mixed_input = jnp.dot(
        normed_one, attn_in_low, preferred_element_type=jnp.float32
    ) + biases_low.astype(jnp.float32)
    query_rows = rotate(
        mixed_input[:, :query_width].reshape(token_rows, QUERY_HEADS, HEAD_SIZE),
        cosine_table,
        sine_table,
    ).astype(jnp.bfloat16)
    key_head_rows = rotate(
        mixed_input[:, query_width : query_width + key_width].reshape(
            token_rows, KEY_VALUE_HEADS, HEAD_SIZE
        ),
        cosine_table,
        sine_table,
    )
    key_head_rows = key_head_rows.astype(jnp.bfloat16).reshape(token_rows, key_width)
    value_head_rows = mixed_input[:, query_width + key_width :].astype(jnp.bfloat16)
    joined_rows = lax.all_gather(
        jnp.concatenate([key_head_rows, value_head_rows], axis=1), "ctx", axis=0, tiled=True
    )
    all_keys = joined_rows[:, :key_width]
    all_values = joined_rows[:, key_width:]
    grouped_queries = query_rows.reshape(token_rows, KEY_VALUE_HEADS, group_count, HEAD_SIZE)

    def block_data(source_keys, values_src, block_index):
        block_offset = block_index * current_key_block
        key_row_matrix = lax.dynamic_slice_in_dim(
            source_keys, block_offset, current_key_block
        ).reshape(current_key_block, KEY_VALUE_HEADS, HEAD_SIZE)
        value_rows = lax.dynamic_slice_in_dim(values_src, block_offset, current_key_block).reshape(
            current_key_block, KEY_VALUE_HEADS, HEAD_SIZE
        )
        doc_slice = lax.dynamic_slice_in_dim(key_doc, block_offset, current_key_block)
        place_slice = lax.dynamic_slice_in_dim(key_place, block_offset, current_key_block)
        scores = (
            jnp.einsum(
                "qhgd,khd->hgqk",
                grouped_queries,
                key_row_matrix,
                preferred_element_type=jnp.float32,
            )
            * 0.125
        )
        allowed = (query_doc[:, None] == doc_slice[None, :]) & (
            place_slice[None, :] <= query_place[:, None]
        )
        return (key_row_matrix, value_rows, scores, allowed)

    def lse_step(block_index, carry):

        def lse_active(state):
            running_max, running_sum = state
            key_row_matrix, value_rows, scores, allowed = block_data(
                all_keys, all_values, block_index
            )
            masked = jnp.where(allowed, scores, -1e30)
            new_max = jnp.maximum(running_max, jnp.max(masked, axis=-1))
            terms = jnp.where(allowed, jnp.exp(masked - new_max[..., None]), 0.0)
            return (new_max, running_sum * jnp.exp(running_max - new_max) + jnp.sum(terms, axis=-1))

        if number_of_blocks == 1:
            return lse_active(carry)
        return lax.cond(
            block_index * current_key_block <= last_place, lse_active, lambda state: state, carry
        )

    initial_maximum = jnp.full((KEY_VALUE_HEADS, group_count, token_rows), -1e30, jnp.float32)
    initial_sum = jnp.zeros((KEY_VALUE_HEADS, group_count, token_rows), jnp.float32)
    final_max, final_sum = over_blocks(
        number_of_blocks, lse_step, (initial_maximum, initial_sum)
    )
    log_total = final_max + jnp.log(final_sum)

    def output_update(block_index, carry):

        def output_active(accum):
            key_row_matrix, value_rows, scores, allowed = block_data(
                all_keys, all_values, block_index
            )
            probs = jnp.where(allowed, jnp.exp(scores - log_total[..., None]), 0.0).astype(
                jnp.bfloat16
            )
            return accum + jnp.einsum(
                "hgqk,khd->qhgd", probs, value_rows, preferred_element_type=jnp.float32
            )

        if number_of_blocks == 1:
            return output_active(carry)
        return lax.cond(
            block_index * current_key_block <= last_place, output_active, lambda accum: accum, carry
        )

    attention_result = over_blocks(
        number_of_blocks,
        output_update,
        jnp.zeros((token_rows, KEY_VALUE_HEADS, group_count, HEAD_SIZE), jnp.float32),
    )
    tied = tie(*own_kinds, *upstream_parts, attention_result)
    own_kinds, upstream_parts = tied[:fsdp_count], tied[fsdp_count:-1]
    attention_result = tied[-1]
    own_kind = by_source(own_kinds, place).reshape(-1, slice_rows)
    other_kind = shift_core(own_kind, ctx_count)
    attended_low = attention_result.reshape(token_rows, query_width).astype(jnp.bfloat16)
    middle_state = inputs + jnp.dot(attended_low, attn_out_low, preferred_element_type=jnp.float32)
    scaled_two, factor_two = rms_parts(middle_state)
    second_normalized = (scaled_two * gain_two).astype(jnp.bfloat16)
    second_parts = share_fsdp(second_normalized, fsdp_count)
    gate_low = jnp.where(core == 0, own_kind, other_kind)
    up_low = jnp.where(core == 0, other_kind, own_kind)
    *second_parts, gate_low, up_low = tie(*second_parts, gate_low, up_low)
    second_all = jnp.concatenate(second_parts, axis=0)
    upstream_all = jnp.concatenate(upstream_parts, axis=0)
    gate_val = jnp.dot(second_all, gate_low, preferred_element_type=jnp.float32)
    up_val = jnp.dot(second_all, up_low, preferred_element_type=jnp.float32)
    sigmoid_val = jax.nn.sigmoid(gate_val)
    silu_val = gate_val * sigmoid_val
    hidden_state = (silu_val * up_val).astype(jnp.bfloat16)
    hidden_grad = times_transposed(upstream_all, mlp_out_low)
    silu_slope = sigmoid_val * (1.0 + gate_val * (1.0 - sigmoid_val))
    gate_grad = (hidden_grad * up_val * silu_slope).astype(jnp.bfloat16)
    up_grad = (hidden_grad * silu_val).astype(jnp.bfloat16)
    normed_two_part = times_transposed(gate_grad, gate_low) + times_transposed(up_grad, up_low)
    normed_two_part = normed_two_part.astype(jnp.bfloat16).reshape(fsdp_count, token_rows, -1)
    normed_two_parts = return_fsdp(normed_two_part, fsdp_count)
    output_part = jnp.dot(hidden_state, mlp_out_low, preferred_element_type=jnp.float32)
    output_part = output_part.astype(jnp.bfloat16).reshape(fsdp_count, token_rows, -1)
    mlp_in_kept = sum_pair(
        transposed_times(second_all, gate_grad).astype(jnp.bfloat16),
        transposed_times(second_all, up_grad).astype(jnp.bfloat16),
        core,
        ctx_count,
    )
    mlp_out_kept = transposed_times(hidden_state, upstream_all).astype(jnp.bfloat16)
    mlp_out_kept = mlp_out_kept.reshape(CHIPS, 2, -1, mlp_out_kept.shape[1])
    mlp_out_kept = sum_pair(mlp_out_kept[:, 0], mlp_out_kept[:, 1], core, ctx_count)
    *normed_two_parts, output_part, mlp_in_kept, mlp_out_kept = tie(
        *normed_two_parts, output_part, mlp_in_kept, mlp_out_kept
    )
    normed_two_grad = total_of(normed_two_parts)
    output_parts = return_fsdp(output_part, fsdp_count)
    mlp_out_parts = send_chips(mlp_out_kept, chip, ctx_count)
    mlp_in_parts = send_chips(by_chip(mlp_in_kept, fsdp_count), chip, ctx_count)
    middle_norm_grad, gain_two_grad = norm_back(
        normed_two_grad, scaled_two, factor_two, gain_two
    )
    middle_grad = upstream.astype(jnp.float32) + middle_norm_grad
    branch_grad = middle_grad.astype(jnp.bfloat16)
    head_gradient = times_transposed(branch_grad, attn_out_low).astype(jnp.bfloat16)
    grouped_head_gradient = head_gradient.reshape(
        token_rows, KEY_VALUE_HEADS, group_count, HEAD_SIZE
    )
    delta = jnp.einsum(
        "qhgd,qhgd->hgq", grouped_head_gradient.astype(jnp.float32), attention_result
    )
    attn_out_part = transposed_times(attended_low, branch_grad).astype(jnp.bfloat16)

    def back_step(block_index, carry):

        def back_active(state):
            query_grad, key_grad, value_grad = state
            key_row_matrix, value_rows, scores, allowed = block_data(
                all_keys, all_values, block_index
            )
            probs = jnp.where(allowed, jnp.exp(scores - log_total[..., None]), 0.0)
            probs_low = probs.astype(jnp.bfloat16)
            prob_grad = jnp.einsum(
                "qhgd,khd->hgqk",
                grouped_head_gradient,
                value_rows,
                preferred_element_type=jnp.float32,
            )
            score_grad = (probs * (prob_grad - delta[..., None])).astype(jnp.bfloat16)
            query_grad = (
                query_grad
                + jnp.einsum(
                    "hgqk,khd->qhgd", score_grad, key_row_matrix, preferred_element_type=jnp.float32
                )
                * 0.125
            )
            key_part = (
                jnp.einsum(
                    "hgqk,qhgd->khd",
                    score_grad,
                    grouped_queries,
                    preferred_element_type=jnp.float32,
                )
                * 0.125
            )
            value_part = jnp.einsum(
                "hgqk,qhgd->khd",
                probs_low,
                grouped_head_gradient,
                preferred_element_type=jnp.float32,
            )
            block_offset = block_index * current_key_block
            key_grad = lax.dynamic_update_slice_in_dim(
                key_grad, key_part.reshape(current_key_block, key_width), block_offset, 0
            )
            value_grad = lax.dynamic_update_slice_in_dim(
                value_grad, value_part.reshape(current_key_block, key_width), block_offset, 0
            )
            return (query_grad, key_grad, value_grad)

        if number_of_blocks == 1:
            return back_active(carry)
        return lax.cond(
            block_index * current_key_block <= last_place, back_active, lambda state: state, carry
        )

    start_state = (
        jnp.zeros((token_rows, KEY_VALUE_HEADS, group_count, HEAD_SIZE), jnp.float32),
        jnp.zeros((seq_len, key_width), jnp.float32),
        jnp.zeros((seq_len, key_width), jnp.float32),
    )
    query_grad, key_grad, value_grad = over_blocks(number_of_blocks, back_step, start_state)
    pair_grad = jnp.concatenate([key_grad, value_grad], axis=1)
    if ctx_count == INNER:
        pair_grad = pair_grad.astype(jnp.bfloat16)
    tied = tie(*output_parts, *mlp_out_parts, *mlp_in_parts, pair_grad)
    output_parts = tied[:fsdp_count]
    mlp_out_parts = tied[fsdp_count : fsdp_count + CHIPS]
    mlp_in_parts = tied[fsdp_count + CHIPS : -1]
    pair_grad = tied[-1]
    output = middle_state + total_of(output_parts)
    if ctx_count == INNER:
        pair_grad = pair_grad.reshape(CHIPS, 2, token_rows, 2 * key_width)
        pair_grad = sum_pair(pair_grad[:, 0], pair_grad[:, 1], core, ctx_count)
        pair_sum = total_of(send_chips(pair_grad, chip, ctx_count))
    else:
        pair_sum = lax.psum_scatter(pair_grad, "ctx", scatter_dimension=0, tiled=True)
    mlp_out_chunk = outer_sum(total_of(mlp_out_parts), ctx_count).astype(jnp.bfloat16)
    mlp_out_grad = lax.all_gather(
        mlp_out_chunk, "ctx", axis=0, axis_index_groups=groups, tiled=True
    ).astype(jnp.float32)
    mlp_in_chunk = outer_sum(total_of(mlp_in_parts), ctx_count).astype(jnp.bfloat16)
    mlp_in_owned = by_source(send_fsdp(mlp_in_chunk, place, fsdp_count), place)
    mlp_in_blocks = lax.all_gather(mlp_in_owned, "ctx", axis=0, axis_index_groups=groups)
    mlp_in_blocks = mlp_in_blocks.reshape(CHIPS, 2, *mlp_in_owned.shape)
    key_total_sum = pair_sum[:, :key_width]
    value_sum = pair_sum[:, key_width:]
    query_low = (
        query_grad.astype(jnp.bfloat16)
        .astype(jnp.float32)
        .reshape(token_rows, QUERY_HEADS, HEAD_SIZE)
    )
    key_reduced = (
        key_total_sum.astype(jnp.bfloat16)
        .astype(jnp.float32)
        .reshape(token_rows, KEY_VALUE_HEADS, HEAD_SIZE)
    )
    value_low = value_sum.astype(jnp.bfloat16).astype(jnp.float32)
    pre_grad = jnp.concatenate(
        [
            unrotate(query_low, cosine_table, sine_table).reshape(token_rows, query_width),
            unrotate(key_reduced, cosine_table, sine_table).reshape(token_rows, key_width),
            value_low,
        ],
        axis=1,
    ).astype(jnp.bfloat16)
    bias_grad = jnp.sum(pre_grad.astype(jnp.float32), axis=0)
    normed_one_grad = times_transposed(pre_grad, attn_in_low)
    input_norm_grad, gain_one_grad = norm_back(
        normed_one_grad, scaled_one, factor_one, gain_one
    )
    input_grad = middle_grad + input_norm_grad
    attn_in_part = transposed_times(normed_one, pre_grad).astype(jnp.bfloat16)
    vectors = jnp.concatenate(
        [
            gain_one_grad.reshape(fsdp_count, -1),
            gain_two_grad.reshape(fsdp_count, -1),
            bias_grad.reshape(fsdp_count, -1),
        ],
        axis=1,
    ).astype(jnp.bfloat16)
    vector_width = vectors.shape[1]
    chip_rows = shard_rows // CHIPS
    attn_part = jnp.concatenate([attn_in_part, attn_out_part], axis=1)
    attn_part = attn_part.reshape(fsdp_count, CHIPS, chip_rows, width)
    extra = jnp.pad(
        vectors[:, None, None], ((0, 0), (0, CHIPS - 1), (0, 7), (0, width - vector_width))
    )
    attn_part = jnp.concatenate([attn_part, extra], axis=2).transpose(1, 0, 2, 3)
    attn_kept = sum_pair(attn_part[..., : width // 2], attn_part[..., width // 2 :], core, ctx_count)
    attn_parts = send_chips(attn_kept, chip, ctx_count)
    upd_mlp_out = adamw(w_mlp_out, mlp_out_grad, first_mlp_out, second_mlp_out, 0.02, 0.1)
    *attn_parts, new_mlp_out, moment_mlp_out, square_mlp_out = tie(*attn_parts, *upd_mlp_out)
    upd_mlp_out = (new_mlp_out, moment_mlp_out, square_mlp_out)
    attn_chunk = outer_sum(total_of(attn_parts), ctx_count).astype(jnp.bfloat16)
    attn_owned = total_of(send_fsdp(attn_chunk, place, fsdp_count)).astype(jnp.bfloat16)
    attn_full = lax.all_gather(attn_owned, "ctx", axis=0, axis_index_groups=groups)
    attn_full = attn_full.reshape(CHIPS, 2, -1, width // 2).transpose(0, 2, 1, 3)
    attn_full = attn_full.reshape(CHIPS, -1, width).astype(jnp.float32)
    attn_rows = attn_full[:, :chip_rows].reshape(shard_rows, width)
    vector = attn_full[0, chip_rows, :vector_width]
    totals = (
        attn_rows[:, :in_width],
        attn_rows[:, in_width:],
        None,
        None,
        vector[: 2 * shard_rows].reshape(2, shard_rows),
        vector[2 * shard_rows :],
    )
    upd_attn_in = adamw(w_attn_in, totals[0], first_attn_in, second_attn_in, 0.02, 0.1)
    upd_attn_out = adamw(w_attn_out, totals[1], first_attn_out, second_attn_out, 0.5, 0.1)
    upd_mlp_in = adamw_blocks(w_mlp_in, mlp_in_blocks, first_mlp_in, second_mlp_in)
    upd_gains = adamw(gains, totals[4], first_gains, second_gains, 0.4, 0.0)
    upd_biases = adamw(biases, totals[5], first_biases, second_biases, 0.02, 0.0)
    return (
        output.astype(jnp.bfloat16)[None],
        input_grad[None],
        upd_attn_in[0],
        upd_attn_in[1],
        upd_attn_in[2],
        upd_attn_out[0],
        upd_attn_out[1],
        upd_attn_out[2],
        upd_mlp_in[0],
        upd_mlp_in[1],
        upd_mlp_in[2],
        upd_mlp_out[0],
        upd_mlp_out[1],
        upd_mlp_out[2],
        upd_gains[0],
        upd_gains[1],
        upd_gains[2],
        upd_biases[0],
        upd_biases[1],
        upd_biases[2],
    )


def solution(mesh):
    return jax.shard_map(
        body,
        mesh=mesh,
        in_specs=(
            P("fsdp", "ctx", None),
            P("fsdp", "ctx", None),
            P("fsdp", None),
            P("fsdp", None),
            P("fsdp", None),
            P("fsdp", None),
            P("fsdp", None),
            P(None, "fsdp"),
            P("fsdp"),
            P("fsdp", None),
            P("fsdp", None),
            P("fsdp", None),
            P("fsdp", None),
            P(None, "fsdp"),
            P("fsdp"),
            P("fsdp", None),
            P("fsdp", None),
            P("fsdp", None),
            P("fsdp", None),
            P(None, "fsdp"),
            P("fsdp"),
        ),
        out_specs=(
            P("fsdp", "ctx", None),
            P("fsdp", "ctx", None),
            P("fsdp", None),
            P("fsdp", None),
            P("fsdp", None),
            P("fsdp", None),
            P("fsdp", None),
            P("fsdp", None),
            P("fsdp", None),
            P("fsdp", None),
            P("fsdp", None),
            P("fsdp", None),
            P("fsdp", None),
            P("fsdp", None),
            P(None, "fsdp"),
            P(None, "fsdp"),
            P(None, "fsdp"),
            P("fsdp"),
            P("fsdp"),
            P("fsdp"),
        ),
        check_vma=False,
    )
```

```python
import jax
import jax.numpy as jnp
from jax import lax
from jax.experimental import pallas as pl
from jax.experimental.pallas import tpu as pltpu
from jax.sharding import PartitionSpec as P

QUERY_HEADS = 14
KEY_VALUE_HEADS = 2
HEAD_SIZE = 64
FF = 4864
NDOC = 4
STEP = 10


norm_eps = 1e-06
rope_base = 1000000.0
beta_one = 0.9
beta_two = 0.999
adam_eps = 1e-08


def rms_parts(values):
    factor = lax.rsqrt(jnp.mean(values * values, axis=-1, keepdims=True) + norm_eps)
    return (values * factor, factor)


def norm_back(incoming, scaled, factor, gain_vec):
    weighted = incoming * gain_vec
    inner = jnp.mean(weighted * scaled, axis=-1, keepdims=True)
    return (factor * (weighted - scaled * inner), jnp.sum(incoming * scaled, axis=0))


def rotate(values, cosine_table, sine_table):
    half_dim = values.shape[-1] // 2
    turned = jnp.concatenate([-values[..., half_dim:], values[..., :half_dim]], axis=-1)
    return values * cosine_table + turned * sine_table


def unrotate(values, cosine_table, sine_table):
    half_dim = values.shape[-1] // 2
    shifted = values * sine_table
    turned = jnp.concatenate([shifted[..., half_dim:], -shifted[..., :half_dim]], axis=-1)
    return values * cosine_table + turned


def times_transposed(left, right):
    return lax.dot_general(
        left, right, (((1,), (1,)), ((), ())), preferred_element_type=jnp.float32
    )


def transposed_times(left, right):
    return lax.dot_general(
        left, right, (((0,), (0,)), ((), ())), preferred_element_type=jnp.float32
    )


def adamw(weight, gradient, first_old, second_old, step_rate, weight_decay):
    first_new = beta_one * first_old + (1.0 - beta_one) * gradient
    second_new = beta_two * second_old + (1.0 - beta_two) * gradient * gradient
    fixed_one = 1.0 - beta_one**STEP
    fixed_two = 1.0 - beta_two**STEP
    step_ratio = first_new / fixed_one / (jnp.sqrt(second_new / fixed_two) + adam_eps)
    return (weight - step_rate * (step_ratio + weight_decay * weight), first_new, second_new)


def over_blocks(count, step, carry):
    if count == 1:
        return step(0, carry)
    return lax.fori_loop(0, count, step, carry)


INNER = 8
CHIPS = 4


def pick(stacked, index):
    return lax.dynamic_index_in_dim(stacked, index, 0, keepdims=False)


def shift_core(values, count):
    return lax.ppermute(values, "ctx", [(i, i ^ 1) for i in range(count)])


def send_chips(stacked, chip, count):
    received = [
        lax.ppermute(pick(stacked, chip ^ d), "ctx", [(i, i ^ (2 * d)) for i in range(count)])
        for d in range(1, CHIPS)
    ]
    return [pick(stacked, chip)] + received


def send_fsdp(stacked, place, count):
    received = [
        lax.ppermute(pick(stacked, place ^ d), "fsdp", [(i, i ^ d) for i in range(count)])
        for d in range(1, count)
    ]
    return [pick(stacked, place)] + received


def share_fsdp(values, count):
    received = [
        lax.ppermute(values, "fsdp", [(i, i ^ d) for i in range(count)]) for d in range(1, count)
    ]
    return [values] + received


def return_fsdp(blocks, count):
    received = [
        lax.ppermute(blocks[d], "fsdp", [(i, i ^ d) for i in range(count)])
        for d in range(1, count)
    ]
    return [blocks[0]] + received


def tie(*values):
    return lax.optimization_barrier(values)


def by_source(entries, place):
    stacked = jnp.stack(entries)
    return jnp.stack([pick(stacked, place ^ j) for j in range(len(entries))])


def total_of(entries):
    out = entries[0].astype(jnp.float32)
    for entry in entries[1:]:
        out = out + entry.astype(jnp.float32)
    return out


def inner_groups(count):
    if count == INNER:
        return None
    return [[g * INNER + i for i in range(INNER)] for g in range(count // INNER)]


def outer_sum(values, count):
    if count == INNER:
        return values
    span = INNER
    while span < count:
        values = values + lax.ppermute(
            values.astype(jnp.bfloat16), "ctx", [(i, i ^ span) for i in range(count)]
        ).astype(jnp.float32)
        span *= 2
    return values


def sum_pair(first_half, second_half, core, count):
    mine = jnp.where(core == 0, first_half, second_half)
    other = jnp.where(core == 0, second_half, first_half)
    arrived = shift_core(other, count)
    return (mine.astype(jnp.float32) + arrived.astype(jnp.float32)).astype(jnp.bfloat16)


def by_chip(kept, fsdp_count):
    rows, width = kept.shape
    part = rows // (fsdp_count * CHIPS)
    return kept.reshape(fsdp_count, CHIPS, part, width).transpose(1, 0, 2, 3)


def adamw_kernel(w_ref, g_ref, first_ref, second_ref, w_out, first_out, second_out):
    slices, width = g_ref.shape[2], g_ref.shape[4]
    for j in range(slices):
        span = slice(j * width, (j + 1) * width)
        new, first_new, second_new = adamw(
            w_ref[:, span],
            g_ref[0, 0, j].astype(jnp.float32),
            first_ref[:, span],
            second_ref[:, span],
            0.02,
            0.1,
        )
        w_out[:, span] = new
        first_out[:, span] = first_new
        second_out[:, span] = second_new


def adamw_blocks(weight, blocks, first_old, second_old):
    chips, kinds, slices, part, width = blocks.shape
    whole = pl.BlockSpec((part, slices * width), lambda i, k: (i, k))
    piece = pl.BlockSpec((1, 1, slices, part, width), lambda i, k: (i, k, 0, 0, 0))
    shape = jax.ShapeDtypeStruct(weight.shape, jnp.float32)
    return pl.pallas_call(
        adamw_kernel,
        grid=(chips, kinds),
        in_specs=[whole, piece, whole, whole],
        out_specs=[whole, whole, whole],
        out_shape=[shape, shape, shape],
        compiler_params=pltpu.CompilerParams(vmem_limit_bytes=40 * 2**20),
        cost_estimate=pl.CostEstimate(
            flops=14 * weight.size, bytes_accessed=26 * weight.size, transcendentals=weight.size
        ),
    )(weight, blocks, first_old, second_old)


def body(
    tokens,
    cotangent,
    doc_lengths,
    w_attn_in,
    w_attn_out,
    w_mlp_in,
    w_mlp_out,
    gains,
    biases,
    first_attn_in,
    first_attn_out,
    first_mlp_in,
    first_mlp_out,
    first_gains,
    first_biases,
    second_attn_in,
    second_attn_out,
    second_mlp_in,
    second_mlp_out,
    second_gains,
    second_biases,
):
    token_rows = tokens.shape[1]
    ctx_count = lax.axis_size("ctx")
    ctx_index = lax.axis_index("ctx")
    seq_len = token_rows * ctx_count
    current_key_block = min(1536, seq_len)
    number_of_blocks = seq_len // current_key_block
    group_count = QUERY_HEADS // KEY_VALUE_HEADS
    query_width = QUERY_HEADS * HEAD_SIZE
    key_width = KEY_VALUE_HEADS * HEAD_SIZE
    inputs = tokens[0].astype(jnp.float32)
    upstream = cotangent[0]
    lengths_row = doc_lengths[0]
    doc_ends = jnp.cumsum(lengths_row)
    doc_starts = doc_ends - lengths_row
    key_place = jnp.arange(seq_len, dtype=jnp.int32)
    key_doc = jnp.sum((key_place[:, None] >= doc_ends[None, :]).astype(jnp.int32), axis=1)
    query_place = ctx_index * token_rows + jnp.arange(token_rows, dtype=jnp.int32)
    query_doc = lax.dynamic_slice_in_dim(key_doc, ctx_index * token_rows, token_rows)
    picked = query_doc[:, None] == jnp.arange(NDOC, dtype=jnp.int32)[None, :]
    inside = query_place - jnp.sum(jnp.where(picked, doc_starts[None, :], 0), axis=1)
    frequency = rope_base ** (-jnp.arange(0, HEAD_SIZE, 2).astype(jnp.float32) / HEAD_SIZE)
    angles = inside.astype(jnp.float32)[:, None] * frequency[None, :]
    angles = jnp.concatenate([angles, angles], axis=-1)
    cosine_table = jnp.cos(angles)[:, None, :]
    sine_table = jnp.sin(angles)[:, None, :]
    last_place = ctx_index * token_rows + token_rows - 1
    fsdp_count = lax.axis_size("fsdp")
    place = lax.axis_index("fsdp")
    core = lax.rem(ctx_index, 2)
    inner = lax.rem(ctx_index, INNER)
    chip = inner // 2
    groups = inner_groups(ctx_count)
    slice_rows = w_mlp_out.shape[0]
    shard_rows = w_attn_in.shape[0]
    in_width = w_attn_in.shape[1]
    part_rows = shard_rows // INNER
    small = jnp.concatenate([gains[0], gains[1], biases]).astype(jnp.bfloat16)
    width = in_width + w_attn_out.shape[1]
    own_part = lax.dynamic_slice_in_dim(w_attn_in, inner * part_rows, part_rows, 0)
    small = jnp.pad(small, (0, in_width - small.shape[0]))
    packed = jnp.concatenate([own_part.astype(jnp.bfloat16), small[None]], axis=0)
    packed = jnp.pad(packed, ((0, 32 - packed.shape[0]), (0, 0)))
    packed = lax.all_gather(packed, "fsdp", axis=0)
    packed, late_mlp_in, late_attn_out, late_upstream = tie(
        packed, w_mlp_in, w_attn_out, upstream
    )
    packed = lax.all_gather(packed, "ctx", axis=0, axis_index_groups=groups)
    attn_in_low = packed[:, :, :part_rows].transpose(1, 0, 2, 3).reshape(-1, in_width)
    out_part = lax.dynamic_slice_in_dim(late_attn_out, inner * part_rows, part_rows, 0)
    out_part = lax.all_gather(out_part.astype(jnp.bfloat16), "fsdp", axis=0)
    out_part = lax.all_gather(out_part, "ctx", axis=0, axis_index_groups=groups)
    attn_out_low = out_part.transpose(1, 0, 2, 3).reshape(-1, w_attn_out.shape[1])
    small_all = packed[0, :, part_rows]
    gains_low = small_all[:, : 2 * shard_rows].reshape(fsdp_count, 2, shard_rows)
    gains_low = gains_low.transpose(1, 0, 2).reshape(2, -1)
    bias_end = 2 * shard_rows + biases.shape[0]
    biases_low = small_all[:, 2 * shard_rows : bias_end].reshape(-1)
    mlp_out_low = w_mlp_out.astype(jnp.bfloat16)
    own_kind = lax.dynamic_slice_in_dim(late_mlp_in, core * FF, FF, 1).astype(jnp.bfloat16)
    own_kind = own_kind.reshape(shard_rows, fsdp_count, slice_rows).transpose(1, 0, 2)
    own_kinds = send_fsdp(own_kind, place, fsdp_count)
    upstream_parts = share_fsdp(late_upstream, fsdp_count)
    gain_one = gains_low[0].astype(jnp.float32)
    gain_two = gains_low[1].astype(jnp.float32)
    scaled_one, factor_one = rms_parts(inputs)
    normed_one = (scaled_one * gain_one).astype(jnp.bfloat16)
    mixed_input = jnp.dot(
        normed_one, attn_in_low, preferred_element_type=jnp.float32
    ) + biases_low.astype(jnp.float32)
    query_rows = rotate(
        mixed_input[:, :query_width].reshape(token_rows, QUERY_HEADS, HEAD_SIZE),
        cosine_table,
        sine_table,
    ).astype(jnp.bfloat16)
    key_head_rows = rotate(
        mixed_input[:, query_width : query_width + key_width].reshape(
            token_rows, KEY_VALUE_HEADS, HEAD_SIZE
        ),
        cosine_table,
        sine_table,
    )
    key_head_rows = key_head_rows.astype(jnp.bfloat16).reshape(token_rows, key_width)
    value_head_rows = mixed_input[:, query_width + key_width :].astype(jnp.bfloat16)
    joined_rows = lax.all_gather(
        jnp.concatenate([key_head_rows, value_head_rows], axis=1), "ctx", axis=0, tiled=True
    )
    all_keys = joined_rows[:, :key_width]
    all_values = joined_rows[:, key_width:]
    grouped_queries = query_rows.reshape(token_rows, KEY_VALUE_HEADS, group_count, HEAD_SIZE)

    def block_data(source_keys, values_src, block_index):
        block_offset = block_index * current_key_block
        key_row_matrix = lax.dynamic_slice_in_dim(
            source_keys, block_offset, current_key_block
        ).reshape(current_key_block, KEY_VALUE_HEADS, HEAD_SIZE)
        value_rows = lax.dynamic_slice_in_dim(values_src, block_offset, current_key_block).reshape(
            current_key_block, KEY_VALUE_HEADS, HEAD_SIZE
        )
        doc_slice = lax.dynamic_slice_in_dim(key_doc, block_offset, current_key_block)
        place_slice = lax.dynamic_slice_in_dim(key_place, block_offset, current_key_block)
        scores = (
            jnp.einsum(
                "qhgd,khd->hgqk",
                grouped_queries,
                key_row_matrix,
                preferred_element_type=jnp.float32,
            )
            * 0.125
        )
        allowed = (query_doc[:, None] == doc_slice[None, :]) & (
            place_slice[None, :] <= query_place[:, None]
        )
        return (key_row_matrix, value_rows, scores, allowed)

    def lse_step(block_index, carry):

        def lse_active(state):
            running_max, running_sum = state
            key_row_matrix, value_rows, scores, allowed = block_data(
                all_keys, all_values, block_index
            )
            masked = jnp.where(allowed, scores, -1e30)
            new_max = jnp.maximum(running_max, jnp.max(masked, axis=-1))
            terms = jnp.where(allowed, jnp.exp(masked - new_max[..., None]), 0.0)
            return (new_max, running_sum * jnp.exp(running_max - new_max) + jnp.sum(terms, axis=-1))

        if number_of_blocks == 1:
            return lse_active(carry)
        return lax.cond(
            block_index * current_key_block <= last_place, lse_active, lambda state: state, carry
        )

    initial_maximum = jnp.full((KEY_VALUE_HEADS, group_count, token_rows), -1e30, jnp.float32)
    initial_sum = jnp.zeros((KEY_VALUE_HEADS, group_count, token_rows), jnp.float32)
    final_max, final_sum = over_blocks(
        number_of_blocks, lse_step, (initial_maximum, initial_sum)
    )
    log_total = final_max + jnp.log(final_sum)

    def output_update(block_index, carry):

        def output_active(accum):
            key_row_matrix, value_rows, scores, allowed = block_data(
                all_keys, all_values, block_index
            )
            probs = jnp.where(allowed, jnp.exp(scores - log_total[..., None]), 0.0).astype(
                jnp.bfloat16
            )
            return accum + jnp.einsum(
                "hgqk,khd->qhgd", probs, value_rows, preferred_element_type=jnp.float32
            )

        if number_of_blocks == 1:
            return output_active(carry)
        return lax.cond(
            block_index * current_key_block <= last_place, output_active, lambda accum: accum, carry
        )

    attention_result = over_blocks(
        number_of_blocks,
        output_update,
        jnp.zeros((token_rows, KEY_VALUE_HEADS, group_count, HEAD_SIZE), jnp.float32),
    )
    tied = tie(*own_kinds, *upstream_parts, attention_result)
    own_kinds, upstream_parts = tied[:fsdp_count], tied[fsdp_count:-1]
    attention_result = tied[-1]
    own_kind = by_source(own_kinds, place).reshape(-1, slice_rows)
    other_kind = shift_core(own_kind, ctx_count)
    attended_low = attention_result.reshape(token_rows, query_width).astype(jnp.bfloat16)
    middle_state = inputs + jnp.dot(attended_low, attn_out_low, preferred_element_type=jnp.float32)
    scaled_two, factor_two = rms_parts(middle_state)
    second_normalized = (scaled_two * gain_two).astype(jnp.bfloat16)
    second_parts = share_fsdp(second_normalized, fsdp_count)
    gate_low = jnp.where(core == 0, own_kind, other_kind)
    up_low = jnp.where(core == 0, other_kind, own_kind)
    *second_parts, gate_low, up_low = tie(*second_parts, gate_low, up_low)
    second_all = jnp.concatenate(second_parts, axis=0)
    upstream_all = jnp.concatenate(upstream_parts, axis=0)
    gate_val = jnp.dot(second_all, gate_low, preferred_element_type=jnp.float32)
    up_val = jnp.dot(second_all, up_low, preferred_element_type=jnp.float32)
    sigmoid_val = jax.nn.sigmoid(gate_val)
    silu_val = gate_val * sigmoid_val
    hidden_state = (silu_val * up_val).astype(jnp.bfloat16)
    hidden_grad = times_transposed(upstream_all, mlp_out_low)
    silu_slope = sigmoid_val * (1.0 + gate_val * (1.0 - sigmoid_val))
    gate_grad = (hidden_grad * up_val * silu_slope).astype(jnp.bfloat16)
    up_grad = (hidden_grad * silu_val).astype(jnp.bfloat16)
    normed_two_part = times_transposed(gate_grad, gate_low) + times_transposed(up_grad, up_low)
    normed_two_part = normed_two_part.astype(jnp.bfloat16).reshape(fsdp_count, token_rows, -1)
    normed_two_parts = return_fsdp(normed_two_part, fsdp_count)
    output_part = jnp.dot(hidden_state, mlp_out_low, preferred_element_type=jnp.float32)
    output_part = output_part.astype(jnp.bfloat16).reshape(fsdp_count, token_rows, -1)
    mlp_in_kept = sum_pair(
        transposed_times(second_all, gate_grad).astype(jnp.bfloat16),
        transposed_times(second_all, up_grad).astype(jnp.bfloat16),
        core,
        ctx_count,
    )
    mlp_out_kept = transposed_times(hidden_state, upstream_all).astype(jnp.bfloat16)
    mlp_out_kept = mlp_out_kept.reshape(CHIPS, 2, -1, mlp_out_kept.shape[1])
    mlp_out_kept = sum_pair(mlp_out_kept[:, 0], mlp_out_kept[:, 1], core, ctx_count)
    *normed_two_parts, output_part, mlp_in_kept, mlp_out_kept = tie(
        *normed_two_parts, output_part, mlp_in_kept, mlp_out_kept
    )
    normed_two_grad = total_of(normed_two_parts)
    output_parts = return_fsdp(output_part, fsdp_count)
    mlp_out_parts = send_chips(mlp_out_kept, chip, ctx_count)
    mlp_in_parts = send_chips(by_chip(mlp_in_kept, fsdp_count), chip, ctx_count)
    middle_norm_grad, gain_two_grad = norm_back(
        normed_two_grad, scaled_two, factor_two, gain_two
    )
    middle_grad = upstream.astype(jnp.float32) + middle_norm_grad
    branch_grad = middle_grad.astype(jnp.bfloat16)
    head_gradient = times_transposed(branch_grad, attn_out_low).astype(jnp.bfloat16)
    grouped_head_gradient = head_gradient.reshape(
        token_rows, KEY_VALUE_HEADS, group_count, HEAD_SIZE
    )
    delta = jnp.einsum(
        "qhgd,qhgd->hgq", grouped_head_gradient.astype(jnp.float32), attention_result
    )
    attn_out_part = transposed_times(attended_low, branch_grad).astype(jnp.bfloat16)

    def back_step(block_index, carry):

        def back_active(state):
            query_grad, key_grad, value_grad = state
            key_row_matrix, value_rows, scores, allowed = block_data(
                all_keys, all_values, block_index
            )
            probs = jnp.where(allowed, jnp.exp(scores - log_total[..., None]), 0.0)
            probs_low = probs.astype(jnp.bfloat16)
            prob_grad = jnp.einsum(
                "qhgd,khd->hgqk",
                grouped_head_gradient,
                value_rows,
                preferred_element_type=jnp.float32,
            )
            score_grad = (probs * (prob_grad - delta[..., None])).astype(jnp.bfloat16)
            query_grad = (
                query_grad
                + jnp.einsum(
                    "hgqk,khd->qhgd", score_grad, key_row_matrix, preferred_element_type=jnp.float32
                )
                * 0.125
            )
            key_part = (
                jnp.einsum(
                    "hgqk,qhgd->khd",
                    score_grad,
                    grouped_queries,
                    preferred_element_type=jnp.float32,
                )
                * 0.125
            )
            value_part = jnp.einsum(
                "hgqk,qhgd->khd",
                probs_low,
                grouped_head_gradient,
                preferred_element_type=jnp.float32,
            )
            block_offset = block_index * current_key_block
            key_grad = lax.dynamic_update_slice_in_dim(
                key_grad, key_part.reshape(current_key_block, key_width), block_offset, 0
            )
            value_grad = lax.dynamic_update_slice_in_dim(
                value_grad, value_part.reshape(current_key_block, key_width), block_offset, 0
            )
            return (query_grad, key_grad, value_grad)

        if number_of_blocks == 1:
            return back_active(carry)
        return lax.cond(
            block_index * current_key_block <= last_place, back_active, lambda state: state, carry
        )

    start_state = (
        jnp.zeros((token_rows, KEY_VALUE_HEADS, group_count, HEAD_SIZE), jnp.float32),
        jnp.zeros((seq_len, key_width), jnp.float32),
        jnp.zeros((seq_len, key_width), jnp.float32),
    )
    query_grad, key_grad, value_grad = over_blocks(number_of_blocks, back_step, start_state)
    pair_grad = jnp.concatenate([key_grad, value_grad], axis=1)
    if ctx_count == INNER:
        pair_grad = pair_grad.astype(jnp.bfloat16)
    tied = tie(*mlp_out_parts, *mlp_in_parts, pair_grad)
    mlp_out_parts, mlp_in_parts, pair_grad = tied[:CHIPS], tied[CHIPS:-1], tied[-1]
    if ctx_count == INNER:
        pair_grad = pair_grad.reshape(CHIPS, 2, token_rows, 2 * key_width)
        pair_grad = sum_pair(pair_grad[:, 0], pair_grad[:, 1], core, ctx_count)
        pair_sum = total_of(send_chips(pair_grad, chip, ctx_count))
    else:
        pair_sum = lax.psum_scatter(pair_grad, "ctx", scatter_dimension=0, tiled=True)
    mlp_out_chunk = outer_sum(total_of(mlp_out_parts), ctx_count).astype(jnp.bfloat16)
    mlp_out_grad = lax.all_gather(
        mlp_out_chunk, "ctx", axis=0, axis_index_groups=groups, tiled=True
    ).astype(jnp.float32)
    mlp_in_chunk = outer_sum(total_of(mlp_in_parts), ctx_count).astype(jnp.bfloat16)
    mlp_in_pieces = send_fsdp(mlp_in_chunk, place, fsdp_count)
    *mlp_in_pieces, pair_sum = tie(*mlp_in_pieces, pair_sum)
    mlp_in_owned = by_source(mlp_in_pieces, place)
    mlp_in_blocks = lax.all_gather(mlp_in_owned, "ctx", axis=0, axis_index_groups=groups)
    mlp_in_blocks = mlp_in_blocks.reshape(CHIPS, 2, *mlp_in_owned.shape)
    key_total_sum = pair_sum[:, :key_width]
    value_sum = pair_sum[:, key_width:]
    query_low = (
        query_grad.astype(jnp.bfloat16)
        .astype(jnp.float32)
        .reshape(token_rows, QUERY_HEADS, HEAD_SIZE)
    )
    key_reduced = (
        key_total_sum.astype(jnp.bfloat16)
        .astype(jnp.float32)
        .reshape(token_rows, KEY_VALUE_HEADS, HEAD_SIZE)
    )
    value_low = value_sum.astype(jnp.bfloat16).astype(jnp.float32)
    pre_grad = jnp.concatenate(
        [
            unrotate(query_low, cosine_table, sine_table).reshape(token_rows, query_width),
            unrotate(key_reduced, cosine_table, sine_table).reshape(token_rows, key_width),
            value_low,
        ],
        axis=1,
    ).astype(jnp.bfloat16)
    bias_grad = jnp.sum(pre_grad.astype(jnp.float32), axis=0)
    normed_one_grad = times_transposed(pre_grad, attn_in_low)
    input_norm_grad, gain_one_grad = norm_back(
        normed_one_grad, scaled_one, factor_one, gain_one
    )
    input_grad = middle_grad + input_norm_grad
    attn_in_part = transposed_times(normed_one, pre_grad).astype(jnp.bfloat16)
    vectors = jnp.concatenate(
        [
            gain_one_grad.reshape(fsdp_count, -1),
            gain_two_grad.reshape(fsdp_count, -1),
            bias_grad.reshape(fsdp_count, -1),
        ],
        axis=1,
    ).astype(jnp.bfloat16)
    vector_width = vectors.shape[1]
    chip_rows = shard_rows // CHIPS
    attn_part = jnp.concatenate([attn_in_part, attn_out_part], axis=1)
    attn_part = attn_part.reshape(fsdp_count, CHIPS, chip_rows, width)
    extra = jnp.pad(
        vectors[:, None, None], ((0, 0), (0, CHIPS - 1), (0, 7), (0, width - vector_width))
    )
    attn_part = jnp.concatenate([attn_part, extra], axis=2).transpose(1, 0, 2, 3)
    attn_kept = sum_pair(attn_part[..., : width // 2], attn_part[..., width // 2 :], core, ctx_count)
    attn_parts = send_chips(attn_kept, chip, ctx_count)
    upd_mlp_out = adamw(w_mlp_out, mlp_out_grad, first_mlp_out, second_mlp_out, 0.02, 0.1)
    tied = tie(*attn_parts, *upd_mlp_out, *output_parts)
    attn_parts, upd_mlp_out, output_parts = tied[:CHIPS], tied[CHIPS:-fsdp_count], tied[-fsdp_count:]
    output = middle_state + total_of(output_parts)
    attn_chunk = outer_sum(total_of(attn_parts), ctx_count).astype(jnp.bfloat16)
    attn_pieces = send_fsdp(attn_chunk, place, fsdp_count)
    *attn_pieces, mlp_in_blocks = tie(*attn_pieces, mlp_in_blocks)
    attn_owned = total_of(attn_pieces).astype(jnp.bfloat16)
    attn_full = lax.all_gather(attn_owned, "ctx", axis=0, axis_index_groups=groups)
    upd_mlp_in = adamw_blocks(w_mlp_in, mlp_in_blocks, first_mlp_in, second_mlp_in)
    attn_full, *upd_mlp_in = tie(attn_full, *upd_mlp_in)
    attn_full = attn_full.reshape(CHIPS, 2, -1, width // 2).transpose(0, 2, 1, 3)
    attn_full = attn_full.reshape(CHIPS, -1, width).astype(jnp.float32)
    attn_rows = attn_full[:, :chip_rows].reshape(shard_rows, width)
    vector = attn_full[0, chip_rows, :vector_width]
    totals = (
        attn_rows[:, :in_width],
        attn_rows[:, in_width:],
        None,
        None,
        vector[: 2 * shard_rows].reshape(2, shard_rows),
        vector[2 * shard_rows :],
    )
    upd_attn_in = adamw(w_attn_in, totals[0], first_attn_in, second_attn_in, 0.02, 0.1)
    upd_attn_out = adamw(w_attn_out, totals[1], first_attn_out, second_attn_out, 0.5, 0.1)
    upd_gains = adamw(gains, totals[4], first_gains, second_gains, 0.4, 0.0)
    upd_biases = adamw(biases, totals[5], first_biases, second_biases, 0.02, 0.0)
    return (
        output.astype(jnp.bfloat16)[None],
        input_grad[None],
        upd_attn_in[0],
        upd_attn_in[1],
        upd_attn_in[2],
        upd_attn_out[0],
        upd_attn_out[1],
        upd_attn_out[2],
        upd_mlp_in[0],
        upd_mlp_in[1],
        upd_mlp_in[2],
        upd_mlp_out[0],
        upd_mlp_out[1],
        upd_mlp_out[2],
        upd_gains[0],
        upd_gains[1],
        upd_gains[2],
        upd_biases[0],
        upd_biases[1],
        upd_biases[2],
    )


def solution(mesh):
    return jax.shard_map(
        body,
        mesh=mesh,
        in_specs=(
            P("fsdp", "ctx", None),
            P("fsdp", "ctx", None),
            P("fsdp", None),
            P("fsdp", None),
            P("fsdp", None),
            P("fsdp", None),
            P("fsdp", None),
            P(None, "fsdp"),
            P("fsdp"),
            P("fsdp", None),
            P("fsdp", None),
            P("fsdp", None),
            P("fsdp", None),
            P(None, "fsdp"),
            P("fsdp"),
            P("fsdp", None),
            P("fsdp", None),
            P("fsdp", None),
            P("fsdp", None),
            P(None, "fsdp"),
            P("fsdp"),
        ),
        out_specs=(
            P("fsdp", "ctx", None),
            P("fsdp", "ctx", None),
            P("fsdp", None),
            P("fsdp", None),
            P("fsdp", None),
            P("fsdp", None),
            P("fsdp", None),
            P("fsdp", None),
            P("fsdp", None),
            P("fsdp", None),
            P("fsdp", None),
            P("fsdp", None),
            P("fsdp", None),
            P("fsdp", None),
            P(None, "fsdp"),
            P(None, "fsdp"),
            P(None, "fsdp"),
            P("fsdp"),
            P("fsdp"),
            P("fsdp"),
        ),
        check_vma=False,
    )
```
